256 devices in a mesh: seq: 32 (over y_hi, z, core), grp: 8 (over y_lo, x).
Axes of the slice: x: 4, y: 4 (y_hi: 2, y_lo: 2; y = y_hi * 2 + y_lo), z: 8, core: 2. Of those that a mesh axis runs over, the one named last changes fastest.
Arguments:
- query_rows: bfloat16 [32768, 2048], P(('seq', 'grp')), may hold values from -24 to 24
- key_rows: bfloat16 [32768, 2048], P(('seq', 'grp')), may hold values from -24 to 24
- value_rows: bfloat16 [32768, 2048], P(('seq', 'grp')), may hold values from -8 to 8
- out_grad: bfloat16 [32768, 2048], P(('seq', 'grp')), may hold values from -6 to 6
Outputs:
- attended: bfloat16 [32768, 2048], P(('seq', 'grp'))
- query_grad: bfloat16 [32768, 2048], P(('seq', 'grp'))
- key_grad: bfloat16 [32768, 2048], P(('seq', 'grp'))
- value_grad: bfloat16 [32768, 2048], P(('seq', 'grp'))
The draws below stay inside these ranges and needn't reach their ends.
All inputs are finite; a program needn't handle non-finite values.
Results may differ from the reference program's by a relative error of at most 0.034.
Values may be sent and summed in bfloat16 or wider, within the bound.
A program may use at most 128 MiB of HBM per device.

```python
import jax
import jax.numpy as jnp
from jax import lax

H = 16
E = 128
BLOCK = 128
LEVELS = 2
TOKENS = 32768


def shared_base(key):
    return jax.random.truncated_normal(key, -4.0, 4.0, (TOKENS, H * E), jnp.float32)


def draw_query_rows(key, part):
    key = jax.random.fold_in(key, 4)
    drawn_rows = 1.5 * jax.random.truncated_normal(key, -4.0, 4.0, (TOKENS, H * E), jnp.float32)
    return drawn_rows.astype(jnp.bfloat16)


def draw_key_rows(key, part):
    base_rows = shared_base(key)
    return base_rows.astype(jnp.bfloat16)


def shard_levels(key, shape, pieces, least, largest):
    gain = 1.0
    for dim, shards_of in pieces:
        steps = jax.random.uniform(jax.random.fold_in(jax.random.fold_in(key, 6), dim), (shards_of,), jnp.float32, least / len(pieces), largest / len(pieces))
        gain = gain * jnp.repeat(jnp.exp(steps), shape[dim] // shards_of).reshape((-1,) + (1,) * (len(shape) - 1 - dim))
    return gain


def scatter_about(own_key, shape, width, most, cuts=(), kind=jnp.bfloat16):
    values = jax.random.normal(own_key, shape, jnp.float32) * width
    if len(cuts) > 0:
        values = shard_levels(own_key, shape, cuts, -0.22, 0.18) * values
    return jnp.clip(values, min=-most, max=most).astype(kind)


def setup_inputs(seed: int = 0) -> dict:
    streams_of = jax.random.split(jax.random.key(seed), 5)
    query_rows = draw_query_rows(jax.random.fold_in(streams_of[4], 71), 0)
    key_rows = draw_key_rows(jax.random.fold_in(streams_of[4], 71), 0)
    value_rows = scatter_about(streams_of[2], (TOKENS, H * E), 2.0, 8.0, ((0, 256),))
    out_grad = scatter_about(streams_of[3], (TOKENS, H * E), 1.0, 6.0, ((0, 256),))
    return dict(query_rows=query_rows, key_rows=key_rows, value_rows=value_rows, out_grad=out_grad)


def level_mask(height, query_pos, key_pos, key_count):
    key_block = jnp.floor_divide(key_pos, BLOCK)
    query_block = jnp.floor_divide(query_pos, BLOCK * 2 ** height)
    inside = (key_pos >= 0) & (key_pos < key_count)
    covered = inside[None, :] & (jnp.abs(key_block[None, :] - query_block[:, None]) <= 1)
    if height > 0:
        finer_block = jnp.floor_divide(query_pos, BLOCK * 2 ** (height - 1))
        pair_block = jnp.floor_divide(2 * key_pos, BLOCK)
        covered = covered & (jnp.abs(pair_block[None, :] - finer_block[:, None]) > 1)
    return covered


def pool_rows(stacked, height):
    if height == 0:
        return stacked
    factor = 2 ** height
    shaped = stacked.reshape(stacked.shape[0], stacked.shape[1] // factor, factor, stacked.shape[2])
    return jnp.mean(shaped.astype(jnp.float32), axis=2).astype(jnp.bfloat16)


def block_terms(query_part, grad_part, key_parts, value_parts, coverage):
    score_scale = E ** -0.5
    scores = []
    for height in range(len(key_parts)):
        raw_score = jnp.einsum("thd,khd->htk", query_part, key_parts[height]) * score_scale
        scores.append(jnp.where(coverage[height][None], raw_score, -jnp.inf))
    peak_score = jnp.max(scores[0], axis=-1)
    for later_score in scores[1:]:
        peak_score = jnp.maximum(peak_score, jnp.max(later_score, axis=-1))
    weights = [(2.0 ** height) * jnp.exp(scores[height] - peak_score[..., None]) for height in range(len(scores))]
    totals = jnp.sum(weights[0], axis=-1)
    for later_weight in weights[1:]:
        totals = totals + jnp.sum(later_weight, axis=-1)
    chances = [entry / totals[..., None] for entry in weights]
    rounded = [entry.astype(jnp.bfloat16) for entry in chances]
    out_sum = jnp.einsum("htk,khd->thd", rounded[0].astype(jnp.float32), value_parts[0])
    for height in range(1, len(scores)):
        out_sum = out_sum + jnp.einsum("htk,khd->thd", rounded[height].astype(jnp.float32), value_parts[height])
    attended = out_sum.astype(jnp.bfloat16)
    row_dot = jnp.sum(grad_part * attended.astype(jnp.float32), axis=-1).T
    query_grad = None
    key_grads = []
    value_grads = []
    for height in range(len(scores)):
        products = jnp.einsum("thd,khd->htk", grad_part, value_parts[height])
        slopes = (chances[height] * (products - row_dot[..., None])).astype(jnp.bfloat16).astype(jnp.float32)
        term = jnp.einsum("htk,khd->thd", slopes, key_parts[height])
        query_grad = term if query_grad is None else query_grad + term
        key_grads.append(jnp.einsum("htk,thd->khd", slopes, query_part) * score_scale)
        value_grads.append(jnp.einsum("htk,thd->khd", rounded[height].astype(jnp.float32), grad_part))
    return attended, query_grad * score_scale, key_grads, value_grads


def reference(query_rows, key_rows, value_rows, out_grad):
    seq_total, features = query_rows.shape
    head_count = features // E
    stacked = jnp.stack([key_rows, value_rows])
    padded = [jnp.pad(pool_rows(stacked, height), ((0, 0), (BLOCK, BLOCK), (0, 0))) for height in range(LEVELS + 1)]
    block_count = seq_total // BLOCK

    def visit_block(running, block_at):
        start_row = block_at * BLOCK
        query_part = lax.dynamic_slice_in_dim(query_rows, start_row, BLOCK, 0).astype(jnp.float32).reshape(BLOCK, head_count, E)
        grad_part = lax.dynamic_slice_in_dim(out_grad, start_row, BLOCK, 0).astype(jnp.float32).reshape(BLOCK, head_count, E)
        query_pos = start_row + jnp.arange(BLOCK, dtype=jnp.int32)
        first_rows = []
        key_parts = []
        value_parts = []
        coverage = []
        for height in range(LEVELS + 1):
            first_row = (block_at // 2 ** height) * BLOCK
            window = lax.dynamic_slice_in_dim(padded[height], first_row, 3 * BLOCK, 1).astype(jnp.float32)
            key_parts.append(window[0].reshape(3 * BLOCK, head_count, E))
            value_parts.append(window[1].reshape(3 * BLOCK, head_count, E))
            key_pos = first_row - BLOCK + jnp.arange(3 * BLOCK, dtype=jnp.int32)
            coverage.append(level_mask(height, query_pos, key_pos, seq_total // 2 ** height))
            first_rows.append(first_row)
        attended, query_grad, key_grads, value_grads = block_terms(query_part, grad_part, key_parts, value_parts, coverage)
        new_state = []
        for height in range(LEVELS + 1):
            change = jnp.stack([key_grads[height], value_grads[height]]).reshape(2, 3 * BLOCK, features)
            current = lax.dynamic_slice_in_dim(running[height], first_rows[height], 3 * BLOCK, 1)
            new_state.append(lax.dynamic_update_slice_in_dim(running[height], current + change, first_rows[height], 1))
        return tuple(new_state), (attended.reshape(BLOCK, features), query_grad.reshape(BLOCK, features).astype(jnp.bfloat16))

    initial = tuple(jnp.zeros(entry.shape, jnp.float32) for entry in padded)
    finished, (attended, query_grad) = lax.scan(visit_block, initial, jnp.arange(block_count, dtype=jnp.int32))
    combined = finished[0][:, BLOCK:-BLOCK]
    for height in range(1, LEVELS + 1):
        combined = combined + jnp.repeat(finished[height][:, BLOCK:-BLOCK] / (2.0 ** height), 2 ** height, axis=1)
    return (attended.reshape(seq_total, features), query_grad.reshape(seq_total, features),
            combined[0].astype(jnp.bfloat16), combined[1].astype(jnp.bfloat16))
```

```python
import functools
import math

import jax
import jax.numpy as jnp
from jax import lax
from jax.experimental import pallas as pl
from jax.experimental.pallas import tpu as pltpu
from jax.sharding import PartitionSpec as P

E = 128
T = 128
STAGES = 2
MESH = pl.DeviceIdType.MESH
NEG = -1e30
SCALE = E ** (-0.5)
LOG2E = 1.4426950408889634

L0 = {-1: 0, 0: 3, 1: 6, 2: 7, 3: 8, 4: 9, 5: 10, 6: 11, 7: 14, 8: 17}
L1 = {-1: 1, 0: 4, 1: 12, 2: 13, 3: 15, 4: 18}
L2 = {-1: 2, 0: 5, 1: 16, 2: 19}
TILES = 20


def own_tile(block):
    return 5 + block - 2 * ((8 - block) // 8) + 2 * (block // 7)


def rows_of(tile):
    if isinstance(tile, int):
        return pl.ds(tile * T, T)
    return pl.ds(pl.multiple_of(tile * T, T), T)


def nt(a, b):
    return lax.dot_general(a, b, (((1,), (1,)), ((), ())), preferred_element_type=jnp.float32)


def nn(a, b):
    return lax.dot_general(a, b, (((1,), (0,)), ((), ())), preferred_element_type=jnp.float32)


def pair_terms(pair, queries, grads, keys, values, bias_prev, bias_next):
    scores = nt(keys, queries)
    products = nt(values, grads)
    zero = jnp.zeros((T, T), jnp.bfloat16)
    chance_cols, slope_cols = [], []
    for half in range(2):
        low, high = (0, T // 2), (T // 2, T // 2)
        whole = (0, T)
        pieces = []
        for at in range(half, half + 3):
            bias = None
            if pair == 0 and at == 0:
                bias = bias_prev
            if pair == 1 and at == 3:
                bias = bias_next
            pieces.append((at, whole, 0, bias))
        pieces.append((4, low if half == 0 else whole, 1, bias_prev if pair == 0 else None))
        pieces.append((5, whole if half == 0 else high, 1, bias_next if pair == 1 else None))
        pieces.append((6, low if pair == 0 else whole, 2, bias_prev))
        pieces.append((7, whole if pair == 0 else high, 2, bias_next))
        lanes = slice(half * T, half * T + T)

        def part(array, piece):
            start = piece[0] * T + piece[1][0]
            return array[start : start + piece[1][1], lanes]

        peak = None
        for piece in pieces:
            top = jnp.max(part(scores, piece).reshape(-1, 8, T), axis=0)
            if piece[3] is not None:
                top = top + piece[3]
            peak = top if peak is None else jnp.maximum(peak, top)
        peak = jnp.max(peak, axis=0, keepdims=True) * (SCALE * LOG2E)
        weights = []
        total = None
        for piece in pieces:
            shift = peak - float(piece[2])
            if piece[3] is not None:
                shift = shift - piece[3]
            weight = jnp.exp2(part(scores, piece) * (SCALE * LOG2E) - shift)
            weights.append(weight)
            term = jnp.sum(weight.reshape(-1, 8, T), axis=0)
            total = term if total is None else total + term
        inverse = 1.0 / jnp.sum(total, axis=0, keepdims=True)
        row_dot = None
        chances = []
        for piece, weight in zip(pieces, weights):
            chance = weight * inverse
            chances.append(chance)
            term = jnp.sum((chance * part(products, piece)).reshape(-1, 8, T), axis=0)
            row_dot = term if row_dot is None else row_dot + term
        row_dot = jnp.sum(row_dot, axis=0, keepdims=True)
        chance_tiles, slope_tiles = [zero] * 8, [zero] * 8
        for piece, chance in zip(pieces, chances):
            slope = (chance * (part(products, piece) - row_dot)).astype(jnp.bfloat16)
            chance = chance.astype(jnp.bfloat16)
            if piece[1] != whole:
                blank = jnp.zeros((T // 2, T), jnp.bfloat16)
                if piece[1] == low:
                    chance = jnp.concatenate([chance, blank], axis=0)
                    slope = jnp.concatenate([slope, blank], axis=0)
                else:
                    chance = jnp.concatenate([blank, chance], axis=0)
                    slope = jnp.concatenate([blank, slope], axis=0)
            chance_tiles[piece[0]] = chance
            slope_tiles[piece[0]] = slope
        chance_cols.append(jnp.concatenate(chance_tiles, axis=0))
        slope_cols.append(jnp.concatenate(slope_tiles, axis=0))
    chance = jnp.concatenate(chance_cols, axis=1)
    slope = jnp.concatenate(slope_cols, axis=1)
    attended = nn(values.T, chance).astype(jnp.bfloat16).T
    query_grad = (nn(keys.T, slope) * SCALE).astype(jnp.bfloat16).T
    return attended, query_grad, nn(slope, queries), nn(chance, grads)


def kernel(groups, q_in, k_in, v_in, g_in, att_out, dq_out, dk_out, dv_out,
           kv, qg, acc, grad_send, grad_recv, result,
           in_send, in_recv, halo_send, halo_recv, back_send, back_recv, out_send, out_recv):
    seq = lax.axis_index("seq")
    me = lax.axis_index("grp")
    nxt = lax.rem(seq + 1, groups)
    prv = lax.rem(seq + groups - 1, groups)

    def peer(step):
        return lax.rem(me // 4 + step // 4, 2) * 4 + lax.rem(lax.rem(me, 4) + lax.rem(step, 4), 4)

    barrier = pltpu.get_barrier_semaphore()

    def greet(step, carry):
        pl.semaphore_signal(barrier, inc=1, device_id=(seq, peer(step)), device_id_type=MESH)
        return carry

    lax.fori_loop(1, 8, greet, 0)
    pl.semaphore_signal(barrier, inc=1, device_id=(nxt, me), device_id_type=MESH)
    pl.semaphore_signal(barrier, inc=1, device_id=(prv, me), device_id_type=MESH)
    pl.semaphore_wait(barrier, 9)

    inputs = (k_in, v_in, q_in, g_in)
    outputs = (att_out, dq_out, dk_out, dv_out)

    def columns(device, stage):
        return pl.ds(pl.multiple_of(device * (STAGES * E) + stage * E, E), E)

    def in_slot(stage, which, block):
        if which < 2:
            return kv.at[stage, which, rows_of(own_tile(block))]
        return qg.at[stage, which - 2, rows_of(block)]

    def in_copy(stage, which, step):
        other = peer(step)
        return pltpu.make_async_remote_copy(
            src_ref=inputs[which].at[:, columns(other, stage)],
            dst_ref=in_slot(stage, which, me),
            send_sem=in_send.at[stage, which, step],
            recv_sem=in_recv.at[stage, which, me],
            device_id=(seq, other),
            device_id_type=MESH,
        )

    def in_local(stage, which):
        return pltpu.make_async_copy(
            inputs[which].at[:, columns(me, stage)],
            in_slot(stage, which, me),
            in_recv.at[stage, which, me],
        )

    for stage in range(STAGES):
        for which in range(4):

            def send(step, carry):
                in_copy(stage, which, step).start()
                return carry

            lax.fori_loop(1, 8, send, 0)
            in_local(stage, which).start()

    def wait_in(stage, which):
        def wait(block, carry):
            slot = in_slot(stage, which, block)
            pltpu.make_async_copy(slot, slot, in_recv.at[stage, which, block]).wait()
            return carry

        lax.fori_loop(0, 8, wait, 0)

    down = lax.broadcasted_iota(jnp.int32, (384, 512), 0)
    along = lax.broadcasted_iota(jnp.int32, (384, 512), 1)
    pool = jnp.where(
        down < 256,
        jnp.where(along // 2 == down, 0.5, 0.0),
        jnp.where(along // 4 == down - 256, 0.25, 0.0),
    ).astype(jnp.bfloat16)
    along = lax.broadcasted_iota(jnp.int32, (512, 384), 1)
    down = lax.broadcasted_iota(jnp.int32, (512, 384), 0)
    unpool = jnp.where(
        along < 256,
        jnp.where(down // 2 == along, 0.5, 0.0),
        jnp.where(down // 4 == along - 256, 0.25, 0.0),
    ).astype(jnp.bfloat16)

    def quad_tiles(quad):
        fine = [L0[4 * quad + i] for i in range(4)]
        return fine, [L1[2 * quad], L1[2 * quad + 1], L2[quad]]

    def halo_copy(stage, side):
        source, target, device = ((14, 0, nxt), (3, 17, prv))[side]
        return pltpu.make_async_remote_copy(
            src_ref=kv.at[stage, :, pl.ds(source * T, 3 * T)],
            dst_ref=kv.at[stage, :, pl.ds(target * T, 3 * T)],
            send_sem=halo_send.at[stage, side],
            recv_sem=halo_recv.at[stage, side],
            device_id=(device, me),
            device_id_type=MESH,
        )

    def back_copy(stage, side):
        return pltpu.make_async_remote_copy(
            src_ref=grad_send.at[stage, side],
            dst_ref=grad_recv.at[stage, side],
            send_sem=back_send.at[stage, side],
            recv_sem=back_recv.at[stage, side],
            device_id=((prv, nxt)[side], me),
            device_id_type=MESH,
        )

    def out_copy(stage, which, step):
        other = peer(step)
        return pltpu.make_async_remote_copy(
            src_ref=result.at[stage, which, rows_of(other)],
            dst_ref=outputs[which].at[:, columns(me, stage)],
            send_sem=out_send.at[stage, which, step],
            recv_sem=out_recv.at[stage, which, me],
            device_id=(seq, other),
            device_id_type=MESH,
        )

    def send_out(stage, which):
        def send(step, carry):
            out_copy(stage, which, step).start()
            return carry

        lax.fori_loop(1, 8, send, 0)
        pltpu.make_async_copy(
            result.at[stage, which, rows_of(me)],
            outputs[which].at[:, columns(me, stage)],
            out_recv.at[stage, which, me],
        ).start()

    def prepare(stage):
        for which in range(2):
            wait_in(stage, which)
        for which in range(2):
            for quad in range(2):
                fine, coarse = quad_tiles(quad)
                rows = jnp.concatenate([kv[stage, which, rows_of(i)] for i in fine], axis=0)
                pooled = nn(pool, rows).astype(jnp.bfloat16)
                for at, tile in enumerate(coarse):
                    kv[stage, which, rows_of(tile)] = pooled[at * T : at * T + T]
        for side in range(2):
            halo_copy(stage, side).start()

    def compute(stage):
        acc[stage] = jnp.zeros(acc.shape[1:], jnp.float32)
        for which in range(2, 4):
            wait_in(stage, which)
        for side in range(2):
            halo_copy(stage, side).wait()

        def one_quad(quad, carry):
            bias_prev = jnp.where((seq == 0) & (quad == 0), NEG, 0.0)
            bias_next = jnp.where((seq == groups - 1) & (quad == 1), NEG, 0.0)
            for pair in range(2):
                names = []
                for table, at0, at1 in (
                    [(L0, 2 * pair + i, 4 + 2 * pair + i) for i in (-1, 0, 1, 2)]
                    + [(L1, pair + i, 2 + pair + i) for i in (-1, 1)]
                    + [(L2, i, 1 + i) for i in (-1, 1)]
                ):
                    first, second = table[at0], table[at1]
                    names.append(first + quad * (second - first))
                keys = jnp.concatenate([kv[stage, 0, rows_of(i)] for i in names], axis=0)
                values = jnp.concatenate([kv[stage, 1, rows_of(i)] for i in names], axis=0)
                rows = pl.ds(pl.multiple_of(quad * 512 + pair * 256, 256), 256)
                attended, query_grad, key_terms, value_terms = pair_terms(
                    pair, qg[stage, 0, rows], qg[stage, 1, rows], keys, values, bias_prev, bias_next
                )
                result[stage, 0, rows] = attended
                result[stage, 1, rows] = query_grad
                for at, tile in enumerate(names):
                    acc[stage, 0, rows_of(tile)] += key_terms[at * T : at * T + T]
                    acc[stage, 1, rows_of(tile)] += value_terms[at * T : at * T + T]
            return carry

        lax.fori_loop(0, 2, one_quad, 0)
        grad_send[stage, 0] = acc[stage, :, pl.ds(0, 3 * T)].astype(jnp.bfloat16)
        grad_send[stage, 1] = acc[stage, :, pl.ds(17 * T, 3 * T)].astype(jnp.bfloat16)
        for side in range(2):
            back_copy(stage, side).start()
        for which in range(2):
            send_out(stage, which)

    def finish(stage):
        for side in range(2):
            back_copy(stage, side).wait()
        acc[stage, :, pl.ds(14 * T, 3 * T)] += grad_recv[stage, 0].astype(jnp.float32)
        acc[stage, :, pl.ds(3 * T, 3 * T)] += grad_recv[stage, 1].astype(jnp.float32)
        for which in range(2):
            for quad in range(2):
                fine, coarse = quad_tiles(quad)
                total = jnp.concatenate([acc[stage, which, rows_of(i)] for i in fine], axis=0)
                pooled = jnp.concatenate([acc[stage, which, rows_of(i)] for i in coarse], axis=0)
                total = total + nn(unpool, pooled.astype(jnp.bfloat16))
                if which == 0:
                    total = total * SCALE
                result[stage, 2 + which, pl.ds(quad * 512, 512)] = total.astype(jnp.bfloat16)
            send_out(stage, 2 + which)

    prepare(0)
    compute(0)
    prepare(1)
    finish(0)
    compute(1)
    finish(1)

    for stage in range(STAGES):
        for which in range(4):

            def wait_sent(step, carry):
                in_copy(stage, which, step).wait_send()
                out_copy(stage, which, step).wait_send()
                return carry

            def wait_landed(block, carry):
                slot = outputs[which].at[:, columns(block, stage)]
                pltpu.make_async_copy(slot, slot, out_recv.at[stage, which, block]).wait()
                return carry

            lax.fori_loop(1, 8, wait_sent, 0)
            lax.fori_loop(0, 8, wait_landed, 0)


def on_device(query_rows, key_rows, value_rows, out_grad):
    groups = lax.axis_size("seq")
    shape = jax.ShapeDtypeStruct(query_rows.shape, jnp.bfloat16)
    anywhere = pl.BlockSpec(memory_space=pl.ANY)
    dma = pltpu.SemaphoreType.DMA
    return pl.pallas_call(
        functools.partial(kernel, groups),
        out_shape=(shape,) * 4,
        in_specs=[anywhere] * 4,
        out_specs=(anywhere,) * 4,
        scratch_shapes=[
            pltpu.VMEM((STAGES, 2, TILES * T, E), jnp.bfloat16),
            pltpu.VMEM((STAGES, 2, 8 * T, E), jnp.bfloat16),
            pltpu.VMEM((STAGES, 2, TILES * T, E), jnp.float32),
            pltpu.VMEM((STAGES, 2, 2, 3 * T, E), jnp.bfloat16),
            pltpu.VMEM((STAGES, 2, 2, 3 * T, E), jnp.bfloat16),
            pltpu.VMEM((STAGES, 4, 8 * T, E), jnp.bfloat16),
            dma((STAGES, 4, 8)),
            dma((STAGES, 4, 8)),
            dma((STAGES, 2)),
            dma((STAGES, 2)),
            dma((STAGES, 2)),
            dma((STAGES, 2)),
            dma((STAGES, 4, 8)),
            dma((STAGES, 4, 8)),
        ],
        compiler_params=pltpu.CompilerParams(
            collective_id=0, has_side_effects=True, vmem_limit_bytes=48 * 2**20
        ),
    )(query_rows, key_rows, value_rows, out_grad)


def solution(mesh):
    placed = P(("seq", "grp"), None)
    return jax.shard_map(
        on_device,
        mesh=mesh,
        in_specs=(placed,) * 4,
        out_specs=(placed,) * 4,
        check_vma=False,
    )
```

```python
import functools
import math

import jax
import jax.numpy as jnp
from jax import lax
from jax.experimental import pallas as pl
from jax.experimental.pallas import tpu as pltpu
from jax.sharding import PartitionSpec as P

E = 128
T = 128
STAGES = 2
MESH = pl.DeviceIdType.MESH
NEG = -1e30
SCALE = E ** (-0.5)
LOG2E = 1.4426950408889634

L0 = {-1: 0, 0: 3, 1: 6, 2: 7, 3: 8, 4: 9, 5: 10, 6: 11, 7: 14, 8: 17}
L1 = {-1: 1, 0: 4, 1: 12, 2: 13, 3: 15, 4: 18}
L2 = {-1: 2, 0: 5, 1: 16, 2: 19}
TILES = 20


def own_tile(block):
    return 5 + block - 2 * ((8 - block) // 8) + 2 * (block // 7)


def rows_of(tile):
    if isinstance(tile, int):
        return pl.ds(tile * T, T)
    return pl.ds(pl.multiple_of(tile * T, T), T)


def nt(a, b):
    return lax.dot_general(a, b, (((1,), (1,)), ((), ())), preferred_element_type=jnp.float32)


def nn(a, b):
    return lax.dot_general(a, b, (((1,), (0,)), ((), ())), preferred_element_type=jnp.float32)


def pair_terms(pair, queries, grads, keys, values, bias_prev, bias_next):
    scores = nt(keys, queries)
    products = nt(values, grads)
    zero = jnp.zeros((T, T), jnp.bfloat16)
    chance_cols, slope_cols = [], []
    for half in range(2):
        low, high = (0, T // 2), (T // 2, T // 2)
        whole = (0, T)
        pieces = []
        for at in range(half, half + 3):
            bias = None
            if pair == 0 and at == 0:
                bias = bias_prev
            if pair == 1 and at == 3:
                bias = bias_next
            pieces.append((at, whole, 0, bias))
        pieces.append((4, low if half == 0 else whole, 1, bias_prev if pair == 0 else None))
        pieces.append((5, whole if half == 0 else high, 1, bias_next if pair == 1 else None))
        pieces.append((6, low if pair == 0 else whole, 2, bias_prev))
        pieces.append((7, whole if pair == 0 else high, 2, bias_next))
        lanes = slice(half * T, half * T + T)

        def part(array, piece):
            start = piece[0] * T + piece[1][0]
            return array[start : start + piece[1][1], lanes]

        peak = None
        for piece in pieces:
            top = jnp.max(part(scores, piece).reshape(-1, 8, T), axis=0)
            if piece[3] is not None:
                top = top + piece[3]
            peak = top if peak is None else jnp.maximum(peak, top)
        peak = jnp.max(peak, axis=0, keepdims=True) * (SCALE * LOG2E)
        weights = []
        total = None
        for piece in pieces:
            shift = peak - float(piece[2])
            if piece[3] is not None:
                shift = shift - piece[3]
            weight = jnp.exp2(part(scores, piece) * (SCALE * LOG2E) - shift)
            weights.append(weight)
            term = jnp.sum(weight.reshape(-1, 8, T), axis=0)
            total = term if total is None else total + term
        inverse = 1.0 / jnp.sum(total, axis=0, keepdims=True)
        row_dot = None
        chances = []
        for piece, weight in zip(pieces, weights):
            chance = weight * inverse
            chances.append(chance)
            term = jnp.sum((chance * part(products, piece)).reshape(-1, 8, T), axis=0)
            row_dot = term if row_dot is None else row_dot + term
        row_dot = jnp.sum(row_dot, axis=0, keepdims=True)
        chance_tiles, slope_tiles = [zero] * 8, [zero] * 8
        for piece, chance in zip(pieces, chances):
            slope = (chance * (part(products, piece) - row_dot)).astype(jnp.bfloat16)
            chance = chance.astype(jnp.bfloat16)
            if piece[1] != whole:
                blank = jnp.zeros((T // 2, T), jnp.bfloat16)
                if piece[1] == low:
                    chance = jnp.concatenate([chance, blank], axis=0)
                    slope = jnp.concatenate([slope, blank], axis=0)
                else:
                    chance = jnp.concatenate([blank, chance], axis=0)
                    slope = jnp.concatenate([blank, slope], axis=0)
            chance_tiles[piece[0]] = chance
            slope_tiles[piece[0]] = slope
        chance_cols.append(jnp.concatenate(chance_tiles, axis=0))
        slope_cols.append(jnp.concatenate(slope_tiles, axis=0))
    chance = jnp.concatenate(chance_cols, axis=1)
    slope = jnp.concatenate(slope_cols, axis=1)
    attended = nn(values.T, chance).astype(jnp.bfloat16).T
    query_grad = (nn(keys.T, slope) * SCALE).astype(jnp.bfloat16).T
    return attended, query_grad, nn(slope, queries), nn(chance, grads)


def kernel(groups, q_in, k_in, v_in, g_in, att_out, dq_out, dk_out, dv_out,
           kv, qg, acc, grad_send, grad_recv, result,
           in_send, in_recv, halo_send, halo_recv, back_send, back_recv, out_send, out_recv):
    seq = lax.axis_index("seq")
    me = lax.axis_index("grp")
    upper = seq // (groups // 2)

    def group(step):
        other = lax.rem(seq + groups + step, groups)
        crossing = lax.rem(upper + other // (groups // 2), 2)
        return other, lax.rem(me + 4 * crossing, 8)

    nxt, prv = group(1), group(-1)

    def peer(step):
        return lax.rem(me // 4 + step // 4, 2) * 4 + lax.rem(lax.rem(me, 4) + lax.rem(step, 4), 4)

    barrier = pltpu.get_barrier_semaphore()

    def greet(step, carry):
        pl.semaphore_signal(barrier, inc=1, device_id=(seq, peer(step)), device_id_type=MESH)
        return carry

    lax.fori_loop(1, 8, greet, 0)
    pl.semaphore_signal(barrier, inc=1, device_id=nxt, device_id_type=MESH)
    pl.semaphore_signal(barrier, inc=1, device_id=prv, device_id_type=MESH)
    pl.semaphore_wait(barrier, 9)

    inputs = (k_in, v_in, q_in, g_in)
    outputs = (att_out, dq_out, dk_out, dv_out)

    def columns(device, stage):
        place = lax.rem(device + 4 * upper, 8)
        return pl.ds(pl.multiple_of(place * (STAGES * E) + stage * E, E), E)

    def in_slot(stage, which, block):
        if which < 2:
            return kv.at[stage, which, rows_of(own_tile(block))]
        return qg.at[stage, which - 2, rows_of(block)]

    def in_copy(stage, which, step):
        other = peer(step)
        return pltpu.make_async_remote_copy(
            src_ref=inputs[which].at[:, columns(other, stage)],
            dst_ref=in_slot(stage, which, me),
            send_sem=in_send.at[stage, which, step],
            recv_sem=in_recv.at[stage, which, me],
            device_id=(seq, other),
            device_id_type=MESH,
        )

    def in_local(stage, which):
        return pltpu.make_async_copy(
            inputs[which].at[:, columns(me, stage)],
            in_slot(stage, which, me),
            in_recv.at[stage, which, me],
        )

    def send_in(stage, which):
        def send(step, carry):
            in_copy(stage, which, step).start()
            return carry

        lax.fori_loop(1, 8, send, 0)
        in_local(stage, which).start()

    for which in range(3):
        send_in(0, which)

    def wait_in(stage, which):
        def wait(block, carry):
            slot = in_slot(stage, which, block)
            pltpu.make_async_copy(slot, slot, in_recv.at[stage, which, block]).wait()
            return carry

        lax.fori_loop(0, 8, wait, 0)

    down = lax.broadcasted_iota(jnp.int32, (384, 512), 0)
    along = lax.broadcasted_iota(jnp.int32, (384, 512), 1)
    pool = jnp.where(
        down < 256,
        jnp.where(along // 2 == down, 0.5, 0.0),
        jnp.where(along // 4 == down - 256, 0.25, 0.0),
    ).astype(jnp.bfloat16)
    along = lax.broadcasted_iota(jnp.int32, (512, 384), 1)
    down = lax.broadcasted_iota(jnp.int32, (512, 384), 0)
    unpool = jnp.where(
        along < 256,
        jnp.where(down // 2 == along, 0.5, 0.0),
        jnp.where(down // 4 == along - 256, 0.25, 0.0),
    ).astype(jnp.bfloat16)

    def quad_tiles(quad):
        fine = [L0[4 * quad + i] for i in range(4)]
        return fine, [L1[2 * quad], L1[2 * quad + 1], L2[quad]]

    def halo_copy(stage, side):
        source, target, device = ((14, 0, nxt), (3, 17, prv))[side]
        return pltpu.make_async_remote_copy(
            src_ref=kv.at[stage, :, pl.ds(source * T, 3 * T)],
            dst_ref=kv.at[stage, :, pl.ds(target * T, 3 * T)],
            send_sem=halo_send.at[stage, side],
            recv_sem=halo_recv.at[stage, side],
            device_id=device,
            device_id_type=MESH,
        )

    def back_copy(stage, side):
        return pltpu.make_async_remote_copy(
            src_ref=grad_send.at[stage, side],
            dst_ref=grad_recv.at[stage, side],
            send_sem=back_send.at[stage, side],
            recv_sem=back_recv.at[stage, side],
            device_id=(prv, nxt)[side],
            device_id_type=MESH,
        )

    def out_copy(stage, which, step):
        other = peer(step)
        return pltpu.make_async_remote_copy(
            src_ref=result.at[stage, which, rows_of(other)],
            dst_ref=outputs[which].at[:, columns(me, stage)],
            send_sem=out_send.at[stage, which, step],
            recv_sem=out_recv.at[stage, which, me],
            device_id=(seq, other),
            device_id_type=MESH,
        )

    def send_out(stage, which, first=0, end=8):
        def send(step, carry):
            @pl.when(step != 0)
            def _():
                out_copy(stage, which, step).start()

            @pl.when(step == 0)
            def _():
                pltpu.make_async_copy(
                    result.at[stage, which, rows_of(me)],
                    outputs[which].at[:, columns(me, stage)],
                    out_recv.at[stage, which, me],
                ).start()

            return carry

        lax.fori_loop(first, end, send, 0)

    def prepare(stage):
        for which in range(2):
            wait_in(stage, which)
            if stage == 0:
                send_in(which, 3 if which == 0 else 0)
        for which in range(2):
            for quad in range(2):
                fine, coarse = quad_tiles(quad)
                rows = jnp.concatenate([kv[stage, which, rows_of(i)] for i in fine], axis=0)
                pooled = nn(pool, rows).astype(jnp.bfloat16)
                for at, tile in enumerate(coarse):
                    kv[stage, which, rows_of(tile)] = pooled[at * T : at * T + T]
        for side in range(2):
            halo_copy(stage, side).start()

    def compute(stage):
        acc[stage] = jnp.zeros(acc.shape[1:], jnp.float32)
        for which in range(2, 4):
            wait_in(stage, which)
            if stage == 0:
                send_in(1, which - 1)
        if stage == 0:
            send_in(1, 3)
        for side in range(2):
            halo_copy(stage, side).wait()

        def one_quad(turn):
            quad = lax.rem(me // 4 + 1 + turn, 2)
            bias_prev = jnp.where((seq == 0) & (quad == 0), NEG, 0.0)
            bias_next = jnp.where((seq == groups - 1) & (quad == 1), NEG, 0.0)
            for pair in range(2):
                names = []
                for table, at0, at1 in (
                    [(L0, 2 * pair + i, 4 + 2 * pair + i) for i in (-1, 0, 1, 2)]
                    + [(L1, pair + i, 2 + pair + i) for i in (-1, 1)]
                    + [(L2, i, 1 + i) for i in (-1, 1)]
                ):
                    first, second = table[at0], table[at1]
                    names.append(first + quad * (second - first))
                keys = jnp.concatenate([kv[stage, 0, rows_of(i)] for i in names], axis=0)
                values = jnp.concatenate([kv[stage, 1, rows_of(i)] for i in names], axis=0)
                rows = pl.ds(pl.multiple_of(quad * 512 + pair * 256, 256), 256)
                attended, query_grad, key_terms, value_terms = pair_terms(
                    pair, qg[stage, 0, rows], qg[stage, 1, rows], keys, values, bias_prev, bias_next
                )
                result[stage, 0, rows] = attended
                result[stage, 1, rows] = query_grad
                for at, tile in enumerate(names):
                    acc[stage, 0, rows_of(tile)] += key_terms[at * T : at * T + T]
                    acc[stage, 1, rows_of(tile)] += value_terms[at * T : at * T + T]
            for which in range(2):
                send_out(stage, which, 4 - 4 * turn, 8 - 4 * turn)

        def first_turn(turn, carry):
            one_quad(turn)
            return carry

        lax.fori_loop(0, 2, first_turn, 0)
        grad_send[stage, 0] = acc[stage, :, pl.ds(0, 3 * T)].astype(jnp.bfloat16)
        grad_send[stage, 1] = acc[stage, :, pl.ds(17 * T, 3 * T)].astype(jnp.bfloat16)
        for side in range(2):
            back_copy(stage, side).start()

    def finish(stage):
        for side in range(2):
            back_copy(stage, side).wait()
        acc[stage, :, pl.ds(14 * T, 3 * T)] += grad_recv[stage, 0].astype(jnp.float32)
        acc[stage, :, pl.ds(3 * T, 3 * T)] += grad_recv[stage, 1].astype(jnp.float32)
        for which in range(2):
            for quad in range(2):
                fine, coarse = quad_tiles(quad)
                total = jnp.concatenate([acc[stage, which, rows_of(i)] for i in fine], axis=0)
                pooled = jnp.concatenate([acc[stage, which, rows_of(i)] for i in coarse], axis=0)
                total = total + nn(unpool, pooled.astype(jnp.bfloat16))
                if which == 0:
                    total = total * SCALE
                result[stage, 2 + which, pl.ds(quad * 512, 512)] = total.astype(jnp.bfloat16)
            send_out(stage, 2 + which)

    prepare(0)
    compute(0)
    prepare(1)
    finish(0)
    compute(1)
    finish(1)

    for stage in range(STAGES):
        for which in range(4):

            def wait_sent(step, carry):
                in_copy(stage, which, step).wait_send()
                out_copy(stage, which, step).wait_send()
                return carry

            def wait_landed(block, carry):
                slot = outputs[which].at[:, columns(block, stage)]
                pltpu.make_async_copy(slot, slot, out_recv.at[stage, which, block]).wait()
                return carry

            lax.fori_loop(1, 8, wait_sent, 0)
            lax.fori_loop(0, 8, wait_landed, 0)


def on_device(query_rows, key_rows, value_rows, out_grad):
    groups = lax.axis_size("seq")
    shape = jax.ShapeDtypeStruct(query_rows.shape, jnp.bfloat16)
    anywhere = pl.BlockSpec(memory_space=pl.ANY)
    dma = pltpu.SemaphoreType.DMA
    return pl.pallas_call(
        functools.partial(kernel, groups),
        out_shape=(shape,) * 4,
        in_specs=[anywhere] * 4,
        out_specs=(anywhere,) * 4,
        scratch_shapes=[
            pltpu.VMEM((STAGES, 2, TILES * T, E), jnp.bfloat16),
            pltpu.VMEM((STAGES, 2, 8 * T, E), jnp.bfloat16),
            pltpu.VMEM((STAGES, 2, TILES * T, E), jnp.float32),
            pltpu.VMEM((STAGES, 2, 2, 3 * T, E), jnp.bfloat16),
            pltpu.VMEM((STAGES, 2, 2, 3 * T, E), jnp.bfloat16),
            pltpu.VMEM((STAGES, 4, 8 * T, E), jnp.bfloat16),
            dma((STAGES, 4, 8)),
            dma((STAGES, 4, 8)),
            dma((STAGES, 2)),
            dma((STAGES, 2)),
            dma((STAGES, 2)),
            dma((STAGES, 2)),
            dma((STAGES, 4, 8)),
            dma((STAGES, 4, 8)),
        ],
        compiler_params=pltpu.CompilerParams(
            collective_id=0, has_side_effects=True, vmem_limit_bytes=63 * 2**20
        ),
    )(query_rows, key_rows, value_rows, out_grad)


def solution(mesh):
    placed = P(("seq", "grp"), None)
    return jax.shard_map(
        on_device,
        mesh=mesh,
        in_specs=(placed,) * 4,
        out_specs=(placed,) * 4,
        check_vma=False,
    )
```

```python
import functools
import math

import jax
import jax.numpy as jnp
from jax import lax
from jax.experimental import pallas as pl
from jax.experimental.pallas import tpu as pltpu
from jax.sharding import PartitionSpec as P

E = 128
T = 128
STAGES = 2
MESH = pl.DeviceIdType.MESH
NEG = -1e30
SCALE = E ** (-0.5)
LOG2E = 1.4426950408889634

L0 = {-1: 0, 0: 3, 1: 6, 2: 7, 3: 8, 4: 9, 5: 10, 6: 11, 7: 14, 8: 17}
L1 = {-1: 1, 0: 4, 1: 12, 2: 13, 3: 15, 4: 18}
L2 = {-1: 2, 0: 5, 1: 16, 2: 19}
TILES = 20


def own_tile(block):
    return 5 + block - 2 * ((8 - block) // 8) + 2 * (block // 7)


def rows_of(tile):
    if isinstance(tile, int):
        return pl.ds(tile * T, T)
    return pl.ds(pl.multiple_of(tile * T, T), T)


def nt(a, b):
    return lax.dot_general(a, b, (((1,), (1,)), ((), ())), preferred_element_type=jnp.float32)


def nn(a, b):
    return lax.dot_general(a, b, (((1,), (0,)), ((), ())), preferred_element_type=jnp.float32)


def pair_terms(pair, queries, grads, keys, values, bias_prev, bias_next):
    scores = nt(keys, queries)
    products = nt(values, grads)
    zero = jnp.zeros((T, T), jnp.bfloat16)
    chance_cols, slope_cols = [], []
    for half in range(2):
        low, high = (0, T // 2), (T // 2, T // 2)
        whole = (0, T)
        pieces = []
        for at in range(half, half + 3):
            bias = None
            if pair == 0 and at == 0:
                bias = bias_prev
            if pair == 1 and at == 3:
                bias = bias_next
            pieces.append((at, whole, 0, bias))
        pieces.append((4, low if half == 0 else whole, 1, bias_prev if pair == 0 else None))
        pieces.append((5, whole if half == 0 else high, 1, bias_next if pair == 1 else None))
        pieces.append((6, low if pair == 0 else whole, 2, bias_prev))
        pieces.append((7, whole if pair == 0 else high, 2, bias_next))
        lanes = slice(half * T, half * T + T)

        def part(array, piece):
            start = piece[0] * T + piece[1][0]
            return array[start : start + piece[1][1], lanes]

        peak = None
        for piece in pieces:
            top = jnp.max(part(scores, piece).reshape(-1, 8, T), axis=0)
            if piece[3] is not None:
                top = top + piece[3]
            peak = top if peak is None else jnp.maximum(peak, top)
        peak = jnp.max(peak, axis=0, keepdims=True) * (SCALE * LOG2E)
        weights = []
        total = row_dot = None
        for piece in pieces:
            shift = peak - float(piece[2])
            if piece[3] is not None:
                shift = shift - piece[3]
            weight = jnp.exp2(part(scores, piece) * (SCALE * LOG2E) - shift)
            weights.append(weight)
            term = jnp.sum(weight.reshape(-1, 8, T), axis=0)
            total = term if total is None else total + term
            term = jnp.sum((weight * part(products, piece)).reshape(-1, 8, T), axis=0)
            row_dot = term if row_dot is None else row_dot + term
        inverse = 1.0 / jnp.sum(total, axis=0, keepdims=True)
        row_dot = jnp.sum(row_dot, axis=0, keepdims=True) * inverse
        chance_tiles, slope_tiles = [zero] * 8, [zero] * 8
        for piece, weight in zip(pieces, weights):
            chance = weight * inverse
            slope = (chance * (part(products, piece) - row_dot)).astype(jnp.bfloat16)
            chance = chance.astype(jnp.bfloat16)
            if piece[1] != whole:
                blank = jnp.zeros((T // 2, T), jnp.bfloat16)
                if piece[1] == low:
                    chance = jnp.concatenate([chance, blank], axis=0)
                    slope = jnp.concatenate([slope, blank], axis=0)
                else:
                    chance = jnp.concatenate([blank, chance], axis=0)
                    slope = jnp.concatenate([blank, slope], axis=0)
            chance_tiles[piece[0]] = chance
            slope_tiles[piece[0]] = slope
        chance_cols.append(jnp.concatenate(chance_tiles, axis=0))
        slope_cols.append(jnp.concatenate(slope_tiles, axis=0))
    chance = jnp.concatenate(chance_cols, axis=1)
    slope = jnp.concatenate(slope_cols, axis=1)
    attended = nn(values.T, chance).astype(jnp.bfloat16).T
    query_grad = (nn(keys.T, slope) * SCALE).astype(jnp.bfloat16).T
    return attended, query_grad, nn(slope, queries), nn(chance, grads)


def kernel(groups, q_in, k_in, v_in, g_in, att_out, dq_out, dk_out, dv_out,
           kv, qg, acc, grad_send, grad_recv, result,
           in_send, in_recv, halo_send, halo_recv, back_send, back_recv, out_send, out_recv):
    seq = lax.axis_index("seq")
    me = lax.axis_index("grp")
    upper = seq // (groups // 2)

    def group(step):
        other = lax.rem(seq + groups + step, groups)
        crossing = lax.rem(upper + other // (groups // 2), 2)
        return other, lax.rem(me + 4 * crossing, 8)

    nxt, prv = group(1), group(-1)

    def peer(step):
        return lax.rem(me // 4 + step // 4, 2) * 4 + lax.rem(lax.rem(me, 4) + lax.rem(step, 4), 4)

    barrier = pltpu.get_barrier_semaphore()

    def greet(step, carry):
        pl.semaphore_signal(barrier, inc=1, device_id=(seq, peer(step)), device_id_type=MESH)
        return carry

    lax.fori_loop(1, 8, greet, 0)
    pl.semaphore_signal(barrier, inc=1, device_id=nxt, device_id_type=MESH)
    pl.semaphore_signal(barrier, inc=1, device_id=prv, device_id_type=MESH)
    pl.semaphore_wait(barrier, 9)

    inputs = (k_in, v_in, q_in, g_in)
    outputs = (att_out, dq_out, dk_out, dv_out)

    def columns(device, stage):
        place = lax.rem(device + 4 * upper, 8)
        return pl.ds(pl.multiple_of(place * (STAGES * E) + stage * E, E), E)

    def in_slot(stage, which, block):
        if which < 2:
            return kv.at[stage, which, rows_of(own_tile(block))]
        return qg.at[stage, which - 2, rows_of(block)]

    def in_copy(stage, which, step):
        other = peer(step)
        return pltpu.make_async_remote_copy(
            src_ref=inputs[which].at[:, columns(other, stage)],
            dst_ref=in_slot(stage, which, me),
            send_sem=in_send.at[stage, which, step],
            recv_sem=in_recv.at[stage, which, me],
            device_id=(seq, other),
            device_id_type=MESH,
        )

    def in_local(stage, which):
        return pltpu.make_async_copy(
            inputs[which].at[:, columns(me, stage)],
            in_slot(stage, which, me),
            in_recv.at[stage, which, me],
        )

    def send_in(stage, which):
        def send(step, carry):
            in_copy(stage, which, step).start()
            return carry

        lax.fori_loop(1, 8, send, 0)
        in_local(stage, which).start()

    for which in range(3):
        send_in(0, which)

    def wait_in(stage, which):
        def wait(block, carry):
            slot = in_slot(stage, which, block)
            pltpu.make_async_copy(slot, slot, in_recv.at[stage, which, block]).wait()
            return carry

        lax.fori_loop(0, 8, wait, 0)

    down = lax.broadcasted_iota(jnp.int32, (384, 512), 0)
    along = lax.broadcasted_iota(jnp.int32, (384, 512), 1)
    pool = jnp.where(
        down < 256,
        jnp.where(along // 2 == down, 0.5, 0.0),
        jnp.where(along // 4 == down - 256, 0.25, 0.0),
    ).astype(jnp.bfloat16)
    along = lax.broadcasted_iota(jnp.int32, (512, 384), 1)
    down = lax.broadcasted_iota(jnp.int32, (512, 384), 0)
    unpool = jnp.where(
        along < 256,
        jnp.where(down // 2 == along, 0.5, 0.0),
        jnp.where(down // 4 == along - 256, 0.25, 0.0),
    ).astype(jnp.bfloat16)

    def quad_tiles(quad):
        fine = [L0[4 * quad + i] for i in range(4)]
        return fine, [L1[2 * quad], L1[2 * quad + 1], L2[quad]]

    def halo_copy(stage, side):
        source, target, device = ((14, 0, nxt), (3, 17, prv))[side]
        return pltpu.make_async_remote_copy(
            src_ref=kv.at[stage, :, pl.ds(source * T, 3 * T)],
            dst_ref=kv.at[stage, :, pl.ds(target * T, 3 * T)],
            send_sem=halo_send.at[stage, side],
            recv_sem=halo_recv.at[stage, side],
            device_id=device,
            device_id_type=MESH,
        )

    def back_copy(stage, side):
        return pltpu.make_async_remote_copy(
            src_ref=grad_send.at[stage, side],
            dst_ref=grad_recv.at[stage, side],
            send_sem=back_send.at[stage, side],
            recv_sem=back_recv.at[stage, side],
            device_id=(prv, nxt)[side],
            device_id_type=MESH,
        )

    def out_copy(stage, which, step):
        other = peer(step)
        return pltpu.make_async_remote_copy(
            src_ref=result.at[stage, which, rows_of(other)],
            dst_ref=outputs[which].at[:, columns(me, stage)],
            send_sem=out_send.at[stage, which, step],
            recv_sem=out_recv.at[stage, which, me],
            device_id=(seq, other),
            device_id_type=MESH,
        )

    def send_out(stage, which, first=0, end=8):
        def send(step, carry):
            @pl.when(step != 0)
            def _():
                out_copy(stage, which, step).start()

            @pl.when(step == 0)
            def _():
                pltpu.make_async_copy(
                    result.at[stage, which, rows_of(me)],
                    outputs[which].at[:, columns(me, stage)],
                    out_recv.at[stage, which, me],
                ).start()

            return carry

        lax.fori_loop(first, end, send, 0)

    def prepare(stage):
        for which in range(2):
            wait_in(stage, which)
            if stage == 0:
                send_in(which, 3 if which == 0 else 0)
        for which in range(2):
            for quad in range(2):
                fine, coarse = quad_tiles(quad)
                rows = jnp.concatenate([kv[stage, which, rows_of(i)] for i in fine], axis=0)
                pooled = nn(pool, rows).astype(jnp.bfloat16)
                for at, tile in enumerate(coarse):
                    kv[stage, which, rows_of(tile)] = pooled[at * T : at * T + T]
        for side in range(2):
            halo_copy(stage, side).start()

    def compute(stage):
        acc[stage] = jnp.zeros(acc.shape[1:], jnp.float32)
        for which in range(2, 4):
            wait_in(stage, which)
            if stage == 0:
                send_in(1, which - 1)
        if stage == 0:
            send_in(1, 3)
        for side in range(2):
            halo_copy(stage, side).wait()

        def one_quad(turn):
            quad = lax.rem(me // 4 + 1 + turn, 2)
            bias_prev = jnp.where((seq == 0) & (quad == 0), NEG, 0.0)
            bias_next = jnp.where((seq == groups - 1) & (quad == 1), NEG, 0.0)
            for pair in range(2):
                names = []
                for table, at0, at1 in (
                    [(L0, 2 * pair + i, 4 + 2 * pair + i) for i in (-1, 0, 1, 2)]
                    + [(L1, pair + i, 2 + pair + i) for i in (-1, 1)]
                    + [(L2, i, 1 + i) for i in (-1, 1)]
                ):
                    first, second = table[at0], table[at1]
                    names.append(first + quad * (second - first))
                keys = jnp.concatenate([kv[stage, 0, rows_of(i)] for i in names], axis=0)
                values = jnp.concatenate([kv[stage, 1, rows_of(i)] for i in names], axis=0)
                rows = pl.ds(pl.multiple_of(quad * 512 + pair * 256, 256), 256)
                attended, query_grad, key_terms, value_terms = pair_terms(
                    pair, qg[stage, 0, rows], qg[stage, 1, rows], keys, values, bias_prev, bias_next
                )
                result[stage, 0, rows] = attended
                result[stage, 1, rows] = query_grad
                for at, tile in enumerate(names):
                    acc[stage, 0, rows_of(tile)] += key_terms[at * T : at * T + T]
                    acc[stage, 1, rows_of(tile)] += value_terms[at * T : at * T + T]
            for which in range(2):
                send_out(stage, which, 4 - 4 * turn, 8 - 4 * turn)

        def first_turn(turn, carry):
            one_quad(turn)
            return carry

        lax.fori_loop(0, 2, first_turn, 0)
        grad_send[stage, 0] = acc[stage, :, pl.ds(0, 3 * T)].astype(jnp.bfloat16)
        grad_send[stage, 1] = acc[stage, :, pl.ds(17 * T, 3 * T)].astype(jnp.bfloat16)
        for side in range(2):
            back_copy(stage, side).start()

    def finish(stage):
        for side in range(2):
            back_copy(stage, side).wait()
        acc[stage, :, pl.ds(14 * T, 3 * T)] += grad_recv[stage, 0].astype(jnp.float32)
        acc[stage, :, pl.ds(3 * T, 3 * T)] += grad_recv[stage, 1].astype(jnp.float32)
        for which in range(2):
            for quad in range(2):
                fine, coarse = quad_tiles(quad)
                total = jnp.concatenate([acc[stage, which, rows_of(i)] for i in fine], axis=0)
                pooled = jnp.concatenate([acc[stage, which, rows_of(i)] for i in coarse], axis=0)
                total = total + nn(unpool, pooled.astype(jnp.bfloat16))
                if which == 0:
                    total = total * SCALE
                result[stage, 2 + which, pl.ds(quad * 512, 512)] = total.astype(jnp.bfloat16)
            send_out(stage, 2 + which)

    prepare(0)
    compute(0)
    prepare(1)
    finish(0)
    compute(1)
    finish(1)

    for stage in range(STAGES):
        for which in range(4):

            def wait_sent(step, carry):
                in_copy(stage, which, step).wait_send()
                out_copy(stage, which, step).wait_send()
                return carry

            def wait_landed(block, carry):
                slot = outputs[which].at[:, columns(block, stage)]
                pltpu.make_async_copy(slot, slot, out_recv.at[stage, which, block]).wait()
                return carry

            lax.fori_loop(1, 8, wait_sent, 0)
            lax.fori_loop(0, 8, wait_landed, 0)


def settle(*refs):
    sources, targets, sem = refs[:4], refs[4:8], refs[8]
    copies = [
        pltpu.make_async_copy(source, target, sem.at[at])
        for at, (source, target) in enumerate(zip(sources, targets))
    ]
    for copy in copies:
        copy.start()
    for copy in copies:
        copy.wait()


def on_device(query_rows, key_rows, value_rows, out_grad):
    groups = lax.axis_size("seq")
    shape = jax.ShapeDtypeStruct(query_rows.shape, jnp.bfloat16)
    anywhere = pl.BlockSpec(memory_space=pl.ANY)
    dma = pltpu.SemaphoreType.DMA
    moved = pl.pallas_call(
        functools.partial(kernel, groups),
        out_shape=(shape,) * 4,
        in_specs=[anywhere] * 4,
        out_specs=(anywhere,) * 4,
        scratch_shapes=[
            pltpu.VMEM((STAGES, 2, TILES * T, E), jnp.bfloat16),
            pltpu.VMEM((STAGES, 2, 8 * T, E), jnp.bfloat16),
            pltpu.VMEM((STAGES, 2, TILES * T, E), jnp.float32),
            pltpu.VMEM((STAGES, 2, 2, 3 * T, E), jnp.bfloat16),
            pltpu.VMEM((STAGES, 2, 2, 3 * T, E), jnp.bfloat16),
            pltpu.VMEM((STAGES, 4, 8 * T, E), jnp.bfloat16),
            dma((STAGES, 4, 8)),
            dma((STAGES, 4, 8)),
            dma((STAGES, 2)),
            dma((STAGES, 2)),
            dma((STAGES, 2)),
            dma((STAGES, 2)),
            dma((STAGES, 4, 8)),
            dma((STAGES, 4, 8)),
        ],
        compiler_params=pltpu.CompilerParams(
            collective_id=0, has_side_effects=True, vmem_limit_bytes=413 * 2**17
        ),
    )(query_rows, key_rows, value_rows, out_grad)
    return pl.pallas_call(
        settle,
        out_shape=(shape,) * 4,
        in_specs=[anywhere] * 4,
        out_specs=(anywhere,) * 4,
        scratch_shapes=[dma((4,))],
        compiler_params=pltpu.CompilerParams(vmem_limit_bytes=2**20),
    )(*moved)


def solution(mesh):
    placed = P(("seq", "grp"), None)
    return jax.shard_map(
        on_device,
        mesh=mesh,
        in_specs=(placed,) * 4,
        out_specs=(placed,) * 4,
        check_vma=False,
    )
```

```python
import functools
import math

import jax
import jax.numpy as jnp
from jax import lax
from jax.experimental import pallas as pl
from jax.experimental.pallas import tpu as pltpu
from jax.sharding import PartitionSpec as P

E = 128
T = 128
STAGES = 2
MESH = pl.DeviceIdType.MESH
NEG = -1e30
SCALE = E ** (-0.5)
LOG2E = 1.4426950408889634

L0 = {-1: 0, 0: 3, 1: 6, 2: 7, 3: 8, 4: 9, 5: 10, 6: 11, 7: 14, 8: 17}
L1 = {-1: 1, 0: 4, 1: 12, 2: 13, 3: 15, 4: 18}
L2 = {-1: 2, 0: 5, 1: 16, 2: 19}
TILES = 20


def own_tile(block):
    return 5 + block - 2 * ((8 - block) // 8) + 2 * (block // 7)


def rows_of(tile):
    if isinstance(tile, int):
        return pl.ds(tile * T, T)
    return pl.ds(pl.multiple_of(tile * T, T), T)


def nt(a, b):
    return lax.dot_general(a, b, (((1,), (1,)), ((), ())), preferred_element_type=jnp.float32)


def nn(a, b):
    return lax.dot_general(a, b, (((1,), (0,)), ((), ())), preferred_element_type=jnp.float32)


def pair_terms(pair, queries, grads, keys, values, bias_prev, bias_next):
    scores = nt(keys, queries)
    products = nt(values, grads)
    zero = jnp.zeros((T, T), jnp.bfloat16)
    chance_cols, slope_cols = [], []
    for half in range(2):
        low, high = (0, T // 2), (T // 2, T // 2)
        whole = (0, T)
        pieces = []
        for at in range(half, half + 3):
            bias = None
            if pair == 0 and at == 0:
                bias = bias_prev
            if pair == 1 and at == 3:
                bias = bias_next
            pieces.append((at, whole, 0, bias))
        pieces.append((4, low if half == 0 else whole, 1, bias_prev if pair == 0 else None))
        pieces.append((5, whole if half == 0 else high, 1, bias_next if pair == 1 else None))
        pieces.append((6, low if pair == 0 else whole, 2, bias_prev))
        pieces.append((7, whole if pair == 0 else high, 2, bias_next))
        lanes = slice(half * T, half * T + T)

        def part(array, piece):
            start = piece[0] * T + piece[1][0]
            return array[start : start + piece[1][1], lanes]

        peak = None
        for piece in pieces:
            top = jnp.max(part(scores, piece).reshape(-1, 8, T), axis=0)
            if piece[3] is not None:
                top = top + piece[3]
            peak = top if peak is None else jnp.maximum(peak, top)
        peak = jnp.max(peak, axis=0, keepdims=True) * (SCALE * LOG2E)
        weights = []
        total = row_dot = None
        for piece in pieces:
            shift = peak - float(piece[2])
            if piece[3] is not None:
                shift = shift - piece[3]
            weight = jnp.exp2(part(scores, piece) * (SCALE * LOG2E) - shift)
            weights.append(weight)
            term = jnp.sum(weight.reshape(-1, 8, T), axis=0)
            total = term if total is None else total + term
            term = jnp.sum((weight * part(products, piece)).reshape(-1, 8, T), axis=0)
            row_dot = term if row_dot is None else row_dot + term
        inverse = 1.0 / jnp.sum(total, axis=0, keepdims=True)
        row_dot = jnp.sum(row_dot, axis=0, keepdims=True) * inverse
        chance_tiles, slope_tiles = [zero] * 8, [zero] * 8
        for piece, weight in zip(pieces, weights):
            chance = weight * inverse
            slope = (chance * (part(products, piece) - row_dot)).astype(jnp.bfloat16)
            chance = chance.astype(jnp.bfloat16)
            if piece[1] != whole:
                blank = jnp.zeros((T // 2, T), jnp.bfloat16)
                if piece[1] == low:
                    chance = jnp.concatenate([chance, blank], axis=0)
                    slope = jnp.concatenate([slope, blank], axis=0)
                else:
                    chance = jnp.concatenate([blank, chance], axis=0)
                    slope = jnp.concatenate([blank, slope], axis=0)
            chance_tiles[piece[0]] = chance
            slope_tiles[piece[0]] = slope
        chance_cols.append(jnp.concatenate(chance_tiles, axis=0))
        slope_cols.append(jnp.concatenate(slope_tiles, axis=0))
    chance = jnp.concatenate(chance_cols, axis=1)
    slope = jnp.concatenate(slope_cols, axis=1)
    attended = nn(values.T, chance).astype(jnp.bfloat16).T
    query_grad = (nn(keys.T, slope) * SCALE).astype(jnp.bfloat16).T
    return attended, query_grad, nn(slope, queries), nn(chance, grads)


def kernel(groups, q_in, k_in, v_in, g_in, att_out, dq_out, dk_out, dv_out,
           kv, qg, acc, grad_send, grad_recv, result,
           in_send, in_recv, halo_send, halo_recv, back_send, back_recv, out_send, out_recv):
    seq = lax.axis_index("seq")
    me = lax.axis_index("grp")
    upper = seq // (groups // 2)

    def group(step):
        other = lax.rem(seq + groups + step, groups)
        crossing = lax.rem(upper + other // (groups // 2), 2)
        return other, lax.rem(me + 4 * crossing, 8)

    nxt, prv = group(1), group(-1)

    peers = [
        lax.rem(me // 4 + step // 4, 2) * 4 + lax.rem(lax.rem(me, 4) + step % 4, 4)
        for step in range(8)
    ]
    peers[0] = me

    barrier = pltpu.get_barrier_semaphore()

    for other in peers[1:]:
        pl.semaphore_signal(barrier, inc=1, device_id=(seq, other), device_id_type=MESH)
    pl.semaphore_signal(barrier, inc=1, device_id=nxt, device_id_type=MESH)
    pl.semaphore_signal(barrier, inc=1, device_id=prv, device_id_type=MESH)
    pl.semaphore_wait(barrier, 9)

    inputs = (k_in, v_in, q_in, g_in)
    outputs = (att_out, dq_out, dk_out, dv_out)
    starts = [lax.rem(other + 4 * upper, 8) * (STAGES * E) for other in peers]

    def columns(step, stage):
        return pl.ds(pl.multiple_of(starts[step] + stage * E, E), E)

    def in_slot(stage, which, block):
        if which < 2:
            return kv.at[stage, which, rows_of(own_tile(block))]
        return qg.at[stage, which - 2, rows_of(block)]

    def in_copy(stage, which, step):
        source = inputs[which].at[:, columns(step, stage)]
        target = in_slot(stage, which, me)
        if step == 0:
            return pltpu.make_async_copy(source, target, in_recv.at[stage, which])
        return pltpu.make_async_remote_copy(
            src_ref=source,
            dst_ref=target,
            send_sem=in_send.at[stage, which],
            recv_sem=in_recv.at[stage, which],
            device_id=(seq, peers[step]),
            device_id_type=MESH,
        )

    def send_in(stage, which):
        for step in (1, 2, 3, 4, 5, 6, 7, 0):
            in_copy(stage, which, step).start()

    for which in range(3):
        send_in(0, which)
    acc[...] = jnp.zeros(acc.shape, jnp.float32)

    def wait_in(stage, which):
        eight = qg.at[stage, 0]
        pltpu.make_async_copy(eight, eight, in_recv.at[stage, which]).wait()

    down = lax.broadcasted_iota(jnp.int32, (384, 512), 0)
    along = lax.broadcasted_iota(jnp.int32, (384, 512), 1)
    pool = jnp.where(
        down < 256,
        jnp.where(along // 2 == down, 0.5, 0.0),
        jnp.where(along // 4 == down - 256, 0.25, 0.0),
    ).astype(jnp.bfloat16)
    along = lax.broadcasted_iota(jnp.int32, (512, 384), 1)
    down = lax.broadcasted_iota(jnp.int32, (512, 384), 0)
    unpool = jnp.where(
        along < 256,
        jnp.where(down // 2 == along, 0.5, 0.0),
        jnp.where(down // 4 == along - 256, 0.25, 0.0),
    ).astype(jnp.bfloat16)

    def quad_tiles(quad):
        fine = [L0[4 * quad + i] for i in range(4)]
        return fine, [L1[2 * quad], L1[2 * quad + 1], L2[quad]]

    def halo_copy(stage, side):
        source, target, device = ((14, 0, nxt), (3, 17, prv))[side]
        return pltpu.make_async_remote_copy(
            src_ref=kv.at[stage, :, pl.ds(source * T, 3 * T)],
            dst_ref=kv.at[stage, :, pl.ds(target * T, 3 * T)],
            send_sem=halo_send.at[stage, side],
            recv_sem=halo_recv.at[stage, side],
            device_id=device,
            device_id_type=MESH,
        )

    def back_copy(stage, side):
        return pltpu.make_async_remote_copy(
            src_ref=grad_send.at[stage, side],
            dst_ref=grad_recv.at[stage, side],
            send_sem=back_send.at[stage, side],
            recv_sem=back_recv.at[stage, side],
            device_id=(prv, nxt)[side],
            device_id_type=MESH,
        )

    def send_out(stage, part, steps):
        for which in (2 * part, 2 * part + 1):
            for step in steps:
                source = result.at[stage, which, rows_of(peers[step])]
                target = outputs[which].at[:, columns(0, stage)]
                if step == 0:
                    pltpu.make_async_copy(source, target, out_recv.at[stage, part]).start()
                    continue
                pltpu.make_async_remote_copy(
                    src_ref=source,
                    dst_ref=target,
                    send_sem=out_send.at[stage, part],
                    recv_sem=out_recv.at[stage, part],
                    device_id=(seq, peers[step]),
                    device_id_type=MESH,
                ).start()

    def prepare(stage):
        for which in range(2):
            wait_in(stage, which)
            if stage == 0:
                send_in(which, 3 if which == 0 else 0)
        for which in range(2):
            for quad in range(2):
                fine, coarse = quad_tiles(quad)
                rows = jnp.concatenate([kv[stage, which, rows_of(i)] for i in fine], axis=0)
                pooled = nn(pool, rows).astype(jnp.bfloat16)
                for at, tile in enumerate(coarse):
                    kv[stage, which, rows_of(tile)] = pooled[at * T : at * T + T]
        for side in range(2):
            halo_copy(stage, side).start()

    def compute(stage):
        for which in range(2, 4):
            wait_in(stage, which)
            if stage == 0:
                send_in(1, which - 1)
        if stage == 0:
            send_in(1, 3)
        for side in range(2):
            halo_copy(stage, side).wait()

        def one_quad(turn):
            quad = lax.rem(me // 4 + 1 + turn, 2)
            bias_prev = jnp.where((seq == 0) & (quad == 0), NEG, 0.0)
            bias_next = jnp.where((seq == groups - 1) & (quad == 1), NEG, 0.0)
            for pair in range(2):
                names = []
                for table, at0, at1 in (
                    [(L0, 2 * pair + i, 4 + 2 * pair + i) for i in (-1, 0, 1, 2)]
                    + [(L1, pair + i, 2 + pair + i) for i in (-1, 1)]
                    + [(L2, i, 1 + i) for i in (-1, 1)]
                ):
                    first, second = table[at0], table[at1]
                    names.append(first + quad * (second - first))
                keys = jnp.concatenate([kv[stage, 0, rows_of(i)] for i in names], axis=0)
                values = jnp.concatenate([kv[stage, 1, rows_of(i)] for i in names], axis=0)
                rows = pl.ds(pl.multiple_of(quad * 512 + pair * 256, 256), 256)
                attended, query_grad, key_terms, value_terms = pair_terms(
                    pair, qg[stage, 0, rows], qg[stage, 1, rows], keys, values, bias_prev, bias_next
                )
                result[stage, 0, rows] = attended
                result[stage, 1, rows] = query_grad
                for at, tile in enumerate(names):
                    acc[stage, 0, rows_of(tile)] += key_terms[at * T : at * T + T]
                    acc[stage, 1, rows_of(tile)] += value_terms[at * T : at * T + T]

            @pl.when(turn == 0)
            def _():
                send_out(stage, 0, (4, 5, 6, 7))

            @pl.when(turn == 1)
            def _():
                send_out(stage, 0, (1, 2, 3, 0))

        def next_turn(turn, carry):
            one_quad(turn)
            return carry

        lax.fori_loop(0, 2, next_turn, 0)
        grad_send[stage, 0] = acc[stage, :, pl.ds(0, 3 * T)].astype(jnp.bfloat16)
        grad_send[stage, 1] = acc[stage, :, pl.ds(17 * T, 3 * T)].astype(jnp.bfloat16)
        for side in range(2):
            back_copy(stage, side).start()

    def finish(stage):
        for side in range(2):
            back_copy(stage, side).wait()
        acc[stage, :, pl.ds(14 * T, 3 * T)] += grad_recv[stage, 0].astype(jnp.float32)
        acc[stage, :, pl.ds(3 * T, 3 * T)] += grad_recv[stage, 1].astype(jnp.float32)
        for which in range(2):
            for quad in range(2):
                fine, coarse = quad_tiles(quad)
                total = jnp.concatenate([acc[stage, which, rows_of(i)] for i in fine], axis=0)
                pooled = jnp.concatenate([acc[stage, which, rows_of(i)] for i in coarse], axis=0)
                total = total + nn(unpool, pooled.astype(jnp.bfloat16))
                if which == 0:
                    total = total * SCALE
                result[stage, 2 + which, pl.ds(quad * 512, 512)] = total.astype(jnp.bfloat16)
        send_out(stage, 1, (4, 5, 6, 7, 1, 2, 3, 0))

    prepare(0)
    compute(0)
    prepare(1)
    finish(0)
    compute(1)
    finish(1)

    for stage in range(STAGES):
        for which in range(4):
            seven = qg.at[stage, 0, pl.ds(0, 7 * T)]
            pltpu.make_async_copy(seven, seven, in_send.at[stage, which]).wait()
        for part in range(2):
            seven = result.at[stage, pl.ds(0, 2), pl.ds(0, 7 * T)]
            pltpu.make_async_copy(seven, seven, out_send.at[stage, part]).wait()
            eight = result.at[stage, pl.ds(0, 2)]
            pltpu.make_async_copy(eight, eight, out_recv.at[stage, part]).wait()


def settle(*refs):
    sources, targets, sem = refs[:4], refs[4:8], refs[8]
    copies = [
        pltpu.make_async_copy(source, target, sem.at[at])
        for at, (source, target) in enumerate(zip(sources, targets))
    ]
    for copy in copies:
        copy.start()
    for copy in copies:
        copy.wait()


def on_device(query_rows, key_rows, value_rows, out_grad):
    groups = lax.axis_size("seq")
    shape = jax.ShapeDtypeStruct(query_rows.shape, jnp.bfloat16)
    anywhere = pl.BlockSpec(memory_space=pl.ANY)
    dma = pltpu.SemaphoreType.DMA
    moved = pl.pallas_call(
        functools.partial(kernel, groups),
        out_shape=(shape,) * 4,
        in_specs=[anywhere] * 4,
        out_specs=(anywhere,) * 4,
        scratch_shapes=[
            pltpu.VMEM((STAGES, 2, TILES * T, E), jnp.bfloat16),
            pltpu.VMEM((STAGES, 2, 8 * T, E), jnp.bfloat16),
            pltpu.VMEM((STAGES, 2, TILES * T, E), jnp.float32),
            pltpu.VMEM((STAGES, 2, 2, 3 * T, E), jnp.bfloat16),
            pltpu.VMEM((STAGES, 2, 2, 3 * T, E), jnp.bfloat16),
            pltpu.VMEM((STAGES, 4, 8 * T, E), jnp.bfloat16),
            dma((STAGES, 4)),
            dma((STAGES, 4)),
            dma((STAGES, 2)),
            dma((STAGES, 2)),
            dma((STAGES, 2)),
            dma((STAGES, 2)),
            dma((STAGES, 2)),
            dma((STAGES, 2)),
        ],
        compiler_params=pltpu.CompilerParams(
            collective_id=0, has_side_effects=True, vmem_limit_bytes=413 * 2**17
        ),
    )(query_rows, key_rows, value_rows, out_grad)
    return pl.pallas_call(
        settle,
        out_shape=(shape,) * 4,
        in_specs=[anywhere] * 4,
        out_specs=(anywhere,) * 4,
        scratch_shapes=[dma((4,))],
        compiler_params=pltpu.CompilerParams(vmem_limit_bytes=2**20),
    )(*moved)


def solution(mesh):
    placed = P(("seq", "grp"), None)
    return jax.shard_map(
        on_device,
        mesh=mesh,
        in_specs=(placed,) * 4,
        out_specs=(placed,) * 4,
        check_vma=False,
    )
```

```python
import functools
import math

import jax
import jax.numpy as jnp
from jax import lax
from jax.experimental import pallas as pl
from jax.experimental.pallas import tpu as pltpu
from jax.sharding import PartitionSpec as P

E = 128
T = 128
STAGES = 2
MESH = pl.DeviceIdType.MESH
NEG = -1e30
SCALE = E ** (-0.5)
LOG2E = 1.4426950408889634

L0 = {-1: 0, 0: 3, 1: 6, 2: 7, 3: 8, 4: 9, 5: 10, 6: 11, 7: 14, 8: 17}
L1 = {-1: 1, 0: 4, 1: 12, 2: 13, 3: 15, 4: 18}
L2 = {-1: 2, 0: 5, 1: 16, 2: 19}
TILES = 20


def own_tile(block):
    return 5 + block - 2 * ((8 - block) // 8) + 2 * (block // 7)


def rows_of(tile):
    if isinstance(tile, int):
        return pl.ds(tile * T, T)
    return pl.ds(pl.multiple_of(tile * T, T), T)


def nt(a, b):
    return lax.dot_general(a, b, (((1,), (1,)), ((), ())), preferred_element_type=jnp.float32)


def nn(a, b):
    return lax.dot_general(a, b, (((1,), (0,)), ((), ())), preferred_element_type=jnp.float32)


def pair_terms(pair, queries, grads, keys, values, bias_prev, bias_next):
    scores = nt(keys, queries)
    products = nt(values, grads)
    zero = jnp.zeros((T, T), jnp.bfloat16)
    chance_cols, slope_cols = [], []
    for half in range(2):
        low, high = (0, T // 2), (T // 2, T // 2)
        whole = (0, T)
        pieces = []
        for at in range(half, half + 3):
            bias = None
            if pair == 0 and at == 0:
                bias = bias_prev
            if pair == 1 and at == 3:
                bias = bias_next
            pieces.append((at, whole, 0, bias))
        pieces.append((4, low if half == 0 else whole, 1, bias_prev if pair == 0 else None))
        pieces.append((5, whole if half == 0 else high, 1, bias_next if pair == 1 else None))
        pieces.append((6, low if pair == 0 else whole, 2, bias_prev))
        pieces.append((7, whole if pair == 0 else high, 2, bias_next))
        lanes = slice(half * T, half * T + T)

        def part(array, piece):
            start = piece[0] * T + piece[1][0]
            return array[start : start + piece[1][1], lanes]

        peak = None
        for piece in pieces:
            top = jnp.max(part(scores, piece).reshape(-1, 8, T), axis=0)
            if piece[3] is not None:
                top = top + piece[3]
            peak = top if peak is None else jnp.maximum(peak, top)
        peak = jnp.max(peak, axis=0, keepdims=True) * (SCALE * LOG2E)
        weights = []
        total = row_dot = None
        for piece in pieces:
            shift = peak - float(piece[2])
            if piece[3] is not None:
                shift = shift - piece[3]
            weight = jnp.exp2(part(scores, piece) * (SCALE * LOG2E) - shift)
            weights.append(weight)
            term = jnp.sum(weight.reshape(-1, 8, T), axis=0)
            total = term if total is None else total + term
            term = jnp.sum((weight * part(products, piece)).reshape(-1, 8, T), axis=0)
            row_dot = term if row_dot is None else row_dot + term
        inverse = 1.0 / jnp.sum(total, axis=0, keepdims=True)
        row_dot = jnp.sum(row_dot, axis=0, keepdims=True) * inverse
        chance_tiles, slope_tiles = [zero] * 8, [zero] * 8
        for piece, weight in zip(pieces, weights):
            chance = weight * inverse
            slope = (chance * (part(products, piece) - row_dot)).astype(jnp.bfloat16)
            chance = chance.astype(jnp.bfloat16)
            if piece[1] != whole:
                blank = jnp.zeros((T // 2, T), jnp.bfloat16)
                if piece[1] == low:
                    chance = jnp.concatenate([chance, blank], axis=0)
                    slope = jnp.concatenate([slope, blank], axis=0)
                else:
                    chance = jnp.concatenate([blank, chance], axis=0)
                    slope = jnp.concatenate([blank, slope], axis=0)
            chance_tiles[piece[0]] = chance
            slope_tiles[piece[0]] = slope
        chance_cols.append(jnp.concatenate(chance_tiles, axis=0))
        slope_cols.append(jnp.concatenate(slope_tiles, axis=0))
    chance = jnp.concatenate(chance_cols, axis=1)
    slope = jnp.concatenate(slope_cols, axis=1)
    attended = nn(values.T, chance).astype(jnp.bfloat16).T
    query_grad = (nn(keys.T, slope) * SCALE).astype(jnp.bfloat16).T
    return attended, query_grad, nn(slope, queries), nn(chance, grads)


def kernel(groups, q_in, k_in, v_in, g_in, att_out, dq_out, dk_out, dv_out,
           kv, qg, acc, grad_send, grad_recv, result,
           in_send, in_recv, halo_send, halo_recv, back_send, back_recv, out_send, out_recv):
    seq = lax.axis_index("seq")
    me = lax.axis_index("grp")
    upper = seq // (groups // 2)

    def group(step):
        other = lax.rem(seq + groups + step, groups)
        crossing = lax.rem(upper + other // (groups // 2), 2)
        return other, lax.rem(me + 4 * crossing, 8)

    nxt, prv = group(1), group(-1)

    peers = [
        lax.rem(me // 4 + step // 4, 2) * 4 + lax.rem(lax.rem(me, 4) + step % 4, 4)
        for step in range(8)
    ]
    peers[0] = me

    barrier = pltpu.get_barrier_semaphore()

    for other in peers[1:]:
        pl.semaphore_signal(barrier, inc=1, device_id=(seq, other), device_id_type=MESH)
    pl.semaphore_signal(barrier, inc=1, device_id=nxt, device_id_type=MESH)
    pl.semaphore_signal(barrier, inc=1, device_id=prv, device_id_type=MESH)
    inputs = (k_in, v_in, q_in, g_in)
    outputs = (att_out, dq_out, dk_out, dv_out)
    starts = [lax.rem(other + 4 * upper, 8) * (STAGES * E) for other in peers]

    def columns(step, stage):
        return pl.ds(pl.multiple_of(starts[step] + stage * E, E), E)

    def in_slot(stage, which, block):
        if which < 2:
            return kv.at[stage, which, rows_of(own_tile(block))]
        return qg.at[stage, which - 2, rows_of(block)]

    def in_copy(stage, which, step):
        source = inputs[which].at[:, columns(step, stage)]
        target = in_slot(stage, which, me)
        if step == 0:
            return pltpu.make_async_copy(source, target, in_recv.at[stage, which])
        return pltpu.make_async_remote_copy(
            src_ref=source,
            dst_ref=target,
            send_sem=in_send.at[stage, which],
            recv_sem=in_recv.at[stage, which],
            device_id=(seq, peers[step]),
            device_id_type=MESH,
        )

    def send_in(stage, which):
        for step in range(1, 8):
            in_copy(stage, which, step).start()

    for stage in range(STAGES):
        for which in range(4):
            in_copy(stage, which, 0).start()
    pl.semaphore_wait(barrier, 9)

    for which in range(3):
        send_in(0, which)
    acc[...] = jnp.zeros(acc.shape, jnp.float32)

    def wait_in(stage, which):
        eight = qg.at[stage, 0]
        pltpu.make_async_copy(eight, eight, in_recv.at[stage, which]).wait()

    down = lax.broadcasted_iota(jnp.int32, (384, 512), 0)
    along = lax.broadcasted_iota(jnp.int32, (384, 512), 1)
    pool = jnp.where(
        down < 256,
        jnp.where(along // 2 == down, 0.5, 0.0),
        jnp.where(along // 4 == down - 256, 0.25, 0.0),
    ).astype(jnp.bfloat16)
    along = lax.broadcasted_iota(jnp.int32, (512, 384), 1)
    down = lax.broadcasted_iota(jnp.int32, (512, 384), 0)
    unpool = jnp.where(
        along < 256,
        jnp.where(down // 2 == along, 0.5, 0.0),
        jnp.where(down // 4 == along - 256, 0.25, 0.0),
    ).astype(jnp.bfloat16)

    def quad_tiles(quad):
        fine = [L0[4 * quad + i] for i in range(4)]
        return fine, [L1[2 * quad], L1[2 * quad + 1], L2[quad]]

    def halo_copy(stage, side):
        source, target, device = ((14, 0, nxt), (3, 17, prv))[side]
        return pltpu.make_async_remote_copy(
            src_ref=kv.at[stage, :, pl.ds(source * T, 3 * T)],
            dst_ref=kv.at[stage, :, pl.ds(target * T, 3 * T)],
            send_sem=halo_send.at[stage, side],
            recv_sem=halo_recv.at[stage, side],
            device_id=device,
            device_id_type=MESH,
        )

    def back_copy(stage, side):
        return pltpu.make_async_remote_copy(
            src_ref=grad_send.at[stage, side],
            dst_ref=grad_recv.at[stage, side],
            send_sem=back_send.at[stage, side],
            recv_sem=back_recv.at[stage, side],
            device_id=(prv, nxt)[side],
            device_id_type=MESH,
        )

    def send_out(stage, arrays, steps):
        for which in arrays:
            part = which // 2
            for step in steps:
                source = result.at[stage, which, rows_of(peers[step])]
                target = outputs[which].at[:, columns(0, stage)]
                if step == 0:
                    pltpu.make_async_copy(source, target, out_recv.at[stage, part]).start()
                    continue
                pltpu.make_async_remote_copy(
                    src_ref=source,
                    dst_ref=target,
                    send_sem=out_send.at[stage, part],
                    recv_sem=out_recv.at[stage, part],
                    device_id=(seq, peers[step]),
                    device_id_type=MESH,
                ).start()

    def prepare(stage):
        for which in range(2):
            wait_in(stage, which)
            if stage == 0:
                send_in(which, 3 if which == 0 else 0)
        for which in range(2):
            for quad in range(2):
                fine, coarse = quad_tiles(quad)
                rows = jnp.concatenate([kv[stage, which, rows_of(i)] for i in fine], axis=0)
                pooled = nn(pool, rows).astype(jnp.bfloat16)
                for at, tile in enumerate(coarse):
                    kv[stage, which, rows_of(tile)] = pooled[at * T : at * T + T]
        for side in range(2):
            halo_copy(stage, side).start()

    def compute(stage):
        for which in range(2, 4):
            wait_in(stage, which)
            if stage == 0:
                send_in(1, which - 1)
        if stage == 0:
            send_in(1, 3)
        for side in range(2):
            halo_copy(stage, side).wait()

        def one_quad(turn):
            quad = lax.rem(me // 4 + 1 + turn, 2)
            bias_prev = jnp.where((seq == 0) & (quad == 0), NEG, 0.0)
            bias_next = jnp.where((seq == groups - 1) & (quad == 1), NEG, 0.0)
            for pair in range(2):
                names = []
                for table, at0, at1 in (
                    [(L0, 2 * pair + i, 4 + 2 * pair + i) for i in (-1, 0, 1, 2)]
                    + [(L1, pair + i, 2 + pair + i) for i in (-1, 1)]
                    + [(L2, i, 1 + i) for i in (-1, 1)]
                ):
                    first, second = table[at0], table[at1]
                    names.append(first + quad * (second - first))
                keys = jnp.concatenate([kv[stage, 0, rows_of(i)] for i in names], axis=0)
                values = jnp.concatenate([kv[stage, 1, rows_of(i)] for i in names], axis=0)
                rows = pl.ds(pl.multiple_of(quad * 512 + pair * 256, 256), 256)
                attended, query_grad, key_terms, value_terms = pair_terms(
                    pair, qg[stage, 0, rows], qg[stage, 1, rows], keys, values, bias_prev, bias_next
                )
                result[stage, 0, rows] = attended
                result[stage, 1, rows] = query_grad
                for at, tile in enumerate(names):
                    acc[stage, 0, rows_of(tile)] += key_terms[at * T : at * T + T]
                    acc[stage, 1, rows_of(tile)] += value_terms[at * T : at * T + T]

            @pl.when(turn == 0)
            def _():
                send_out(stage, (0, 1), (4, 5, 6, 7))

            @pl.when(turn == 1)
            def _():
                send_out(stage, (0, 1), (1, 2, 3, 0))

        def next_turn(turn, carry):
            one_quad(turn)
            return carry

        lax.fori_loop(0, 2, next_turn, 0)
        grad_send[stage, 0] = acc[stage, :, pl.ds(0, 3 * T)].astype(jnp.bfloat16)
        grad_send[stage, 1] = acc[stage, :, pl.ds(17 * T, 3 * T)].astype(jnp.bfloat16)
        for side in range(2):
            back_copy(stage, side).start()

    def finish(stage):
        for side in range(2):
            back_copy(stage, side).wait()
        acc[stage, :, pl.ds(14 * T, 3 * T)] += grad_recv[stage, 0].astype(jnp.float32)
        acc[stage, :, pl.ds(3 * T, 3 * T)] += grad_recv[stage, 1].astype(jnp.float32)
        for which in range(2):
            for quad in range(2):
                fine, coarse = quad_tiles(quad)
                total = jnp.concatenate([acc[stage, which, rows_of(i)] for i in fine], axis=0)
                pooled = jnp.concatenate([acc[stage, which, rows_of(i)] for i in coarse], axis=0)
                total = total + nn(unpool, pooled.astype(jnp.bfloat16))
                if which == 0:
                    total = total * SCALE
                result[stage, 2 + which, pl.ds(quad * 512, 512)] = total.astype(jnp.bfloat16)
            send_out(stage, (2 + which,), (4, 5, 6, 7, 1, 2, 3, 0))

    prepare(0)
    compute(0)
    prepare(1)
    finish(0)
    compute(1)
    finish(1)

    for stage in range(STAGES):
        for which in range(4):
            seven = qg.at[stage, 0, pl.ds(0, 7 * T)]
            pltpu.make_async_copy(seven, seven, in_send.at[stage, which]).wait()
        for part in range(2):
            seven = result.at[stage, pl.ds(0, 2), pl.ds(0, 7 * T)]
            pltpu.make_async_copy(seven, seven, out_send.at[stage, part]).wait()
            eight = result.at[stage, pl.ds(0, 2)]
            pltpu.make_async_copy(eight, eight, out_recv.at[stage, part]).wait()


def settle(*refs):
    sources, targets, sem = refs[:4], refs[4:8], refs[8]
    copies = [
        pltpu.make_async_copy(source.at[rows], target.at[rows], sem.at[at, half])
        for at, (source, target) in enumerate(zip(sources, targets))
        for half, rows in enumerate((pl.ds(0, 64), pl.ds(64, 64)))
    ]
    for copy in copies:
        copy.start()
    for copy in copies:
        copy.wait()


def on_device(query_rows, key_rows, value_rows, out_grad):
    groups = lax.axis_size("seq")
    shape = jax.ShapeDtypeStruct(query_rows.shape, jnp.bfloat16)
    anywhere = pl.BlockSpec(memory_space=pl.ANY)
    dma = pltpu.SemaphoreType.DMA
    moved = pl.pallas_call(
        functools.partial(kernel, groups),
        out_shape=(shape,) * 4,
        in_specs=[anywhere] * 4,
        out_specs=(anywhere,) * 4,
        scratch_shapes=[
            pltpu.VMEM((STAGES, 2, TILES * T, E), jnp.bfloat16),
            pltpu.VMEM((STAGES, 2, 8 * T, E), jnp.bfloat16),
            pltpu.VMEM((STAGES, 2, TILES * T, E), jnp.float32),
            pltpu.VMEM((STAGES, 2, 2, 3 * T, E), jnp.bfloat16),
            pltpu.VMEM((STAGES, 2, 2, 3 * T, E), jnp.bfloat16),
            pltpu.VMEM((STAGES, 4, 8 * T, E), jnp.bfloat16),
            dma((STAGES, 4)),
            dma((STAGES, 4)),
            dma((STAGES, 2)),
            dma((STAGES, 2)),
            dma((STAGES, 2)),
            dma((STAGES, 2)),
            dma((STAGES, 2)),
            dma((STAGES, 2)),
        ],
        compiler_params=pltpu.CompilerParams(
            collective_id=0, has_side_effects=True, vmem_limit_bytes=413 * 2**17
        ),
    )(query_rows, key_rows, value_rows, out_grad)
    return pl.pallas_call(
        settle,
        out_shape=(shape,) * 4,
        in_specs=[anywhere] * 4,
        out_specs=(anywhere,) * 4,
        scratch_shapes=[dma((4, 2))],
        compiler_params=pltpu.CompilerParams(vmem_limit_bytes=2**20),
    )(*moved)


def solution(mesh):
    placed = P(("seq", "grp"), None)
    return jax.shard_map(
        on_device,
        mesh=mesh,
        in_specs=(placed,) * 4,
        out_specs=(placed,) * 4,
        check_vma=False,
    )
```

```python
import functools
import math

import jax
import jax.numpy as jnp
from jax import lax
from jax.experimental import pallas as pl
from jax.experimental.pallas import tpu as pltpu
from jax.sharding import PartitionSpec as P

E = 128
T = 128
STAGES = 2
MESH = pl.DeviceIdType.MESH
NEG = -1e30
SCALE = E ** (-0.5)
LOG2E = 1.4426950408889634

L0 = {-1: 0, 0: 3, 1: 6, 2: 7, 3: 8, 4: 9, 5: 10, 6: 11, 7: 14, 8: 17}
L1 = {-1: 1, 0: 4, 1: 12, 2: 13, 3: 15, 4: 18}
L2 = {-1: 2, 0: 5, 1: 16, 2: 19}
TILES = 20


def own_tile(block):
    return 5 + block - 2 * ((8 - block) // 8) + 2 * (block // 7)


def rows_of(tile):
    if isinstance(tile, int):
        return pl.ds(tile * T, T)
    return pl.ds(pl.multiple_of(tile * T, T), T)


def nt(a, b):
    return lax.dot_general(a, b, (((1,), (1,)), ((), ())), preferred_element_type=jnp.float32)


def nn(a, b):
    return lax.dot_general(a, b, (((1,), (0,)), ((), ())), preferred_element_type=jnp.float32)


def pair_terms(pair, queries, grads, keys, values, bias_prev, bias_next):
    scores = nt(keys, queries)
    products = nt(values, grads)
    zero = jnp.zeros((T, T), jnp.bfloat16)
    chance_cols, slope_cols = [], []
    for half in range(2):
        low, high = (0, T // 2), (T // 2, T // 2)
        whole = (0, T)
        pieces = []
        for at in range(half, half + 3):
            bias = None
            if pair == 0 and at == 0:
                bias = bias_prev
            if pair == 1 and at == 3:
                bias = bias_next
            pieces.append((at, whole, 0, bias))
        pieces.append((4, low if half == 0 else whole, 1, bias_prev if pair == 0 else None))
        pieces.append((5, whole if half == 0 else high, 1, bias_next if pair == 1 else None))
        pieces.append((6, low if pair == 0 else whole, 2, bias_prev))
        pieces.append((7, whole if pair == 0 else high, 2, bias_next))
        lanes = slice(half * T, half * T + T)

        def part(array, piece):
            start = piece[0] * T + piece[1][0]
            return array[start : start + piece[1][1], lanes]

        peak = None
        for piece in pieces:
            top = jnp.max(part(scores, piece).reshape(-1, 8, T), axis=0)
            if piece[3] is not None:
                top = top + piece[3]
            peak = top if peak is None else jnp.maximum(peak, top)
        peak = jnp.max(peak, axis=0, keepdims=True) * (SCALE * LOG2E)
        weights = []
        total = row_dot = None
        for piece in pieces:
            shift = peak - float(piece[2])
            if piece[3] is not None:
                shift = shift - piece[3]
            weight = jnp.exp2(part(scores, piece) * (SCALE * LOG2E) - shift)
            weights.append(weight)
            term = jnp.sum(weight.reshape(-1, 8, T), axis=0)
            total = term if total is None else total + term
            term = jnp.sum((weight * part(products, piece)).reshape(-1, 8, T), axis=0)
            row_dot = term if row_dot is None else row_dot + term
        inverse = 1.0 / jnp.sum(total, axis=0, keepdims=True)
        row_dot = jnp.sum(row_dot, axis=0, keepdims=True) * inverse
        chance_tiles, slope_tiles = [zero] * 8, [zero] * 8
        for piece, weight in zip(pieces, weights):
            chance = weight * inverse
            slope = (chance * (part(products, piece) - row_dot)).astype(jnp.bfloat16)
            chance = chance.astype(jnp.bfloat16)
            if piece[1] != whole:
                blank = jnp.zeros((T // 2, T), jnp.bfloat16)
                if piece[1] == low:
                    chance = jnp.concatenate([chance, blank], axis=0)
                    slope = jnp.concatenate([slope, blank], axis=0)
                else:
                    chance = jnp.concatenate([blank, chance], axis=0)
                    slope = jnp.concatenate([blank, slope], axis=0)
            chance_tiles[piece[0]] = chance
            slope_tiles[piece[0]] = slope
        chance_cols.append(jnp.concatenate(chance_tiles, axis=0))
        slope_cols.append(jnp.concatenate(slope_tiles, axis=0))
    chance = jnp.concatenate(chance_cols, axis=1)
    slope = jnp.concatenate(slope_cols, axis=1)
    attended = nn(values.T, chance).astype(jnp.bfloat16).T
    query_grad = (nn(keys.T, slope) * SCALE).astype(jnp.bfloat16).T
    return attended, query_grad, nn(slope, queries), nn(chance, grads)


def kernel(groups, q_in, k_in, v_in, g_in, att_out, dq_out, dk_out, dv_out,
           kv, qg, acc, grad_send, grad_recv, result,
           in_send, in_recv, halo_send, halo_recv, back_send, back_recv, out_send, out_recv):
    seq = lax.axis_index("seq")
    me = lax.axis_index("grp")
    upper = seq // (groups // 2)

    def group(step):
        other = lax.rem(seq + groups + step, groups)
        crossing = lax.rem(upper + other // (groups // 2), 2)
        return other, lax.rem(me + 4 * crossing, 8)

    nxt, prv = group(1), group(-1)

    peers = [
        lax.rem(me // 4 + step // 4, 2) * 4 + lax.rem(lax.rem(me, 4) + step % 4, 4)
        for step in range(8)
    ]
    peers[0] = me

    barrier = pltpu.get_barrier_semaphore()

    for other in peers[1:]:
        pl.semaphore_signal(barrier, inc=1, device_id=(seq, other), device_id_type=MESH)
    pl.semaphore_signal(barrier, inc=1, device_id=nxt, device_id_type=MESH)
    pl.semaphore_signal(barrier, inc=1, device_id=prv, device_id_type=MESH)
    inputs = (k_in, v_in, q_in, g_in)
    outputs = (att_out, dq_out, dk_out, dv_out)
    starts = [lax.rem(other + 4 * upper, 8) * (STAGES * E) for other in peers]

    def columns(step, stage):
        return pl.ds(pl.multiple_of(starts[step] + stage * E, E), E)

    def in_slot(stage, which, block):
        if which < 2:
            return kv.at[stage, which, rows_of(own_tile(block))]
        return qg.at[stage, which - 2, rows_of(block)]

    def in_copy(stage, which, step):
        source = inputs[which].at[:, columns(step, stage)]
        target = in_slot(stage, which, me)
        if step == 0:
            return pltpu.make_async_copy(source, target, in_recv.at[stage, which])
        return pltpu.make_async_remote_copy(
            src_ref=source,
            dst_ref=target,
            send_sem=in_send.at[stage, which],
            recv_sem=in_recv.at[stage, which],
            device_id=(seq, peers[step]),
            device_id_type=MESH,
        )

    def send_in(stage, which):
        for step in range(1, 8):
            in_copy(stage, which, step).start()

    for stage in range(STAGES):
        for which in range(4):
            in_copy(stage, which, 0).start()
    pl.semaphore_wait(barrier, 9)

    for which in range(3):
        send_in(0, which)
    acc[...] = jnp.zeros(acc.shape, jnp.float32)

    def wait_in(stage, which):
        eight = qg.at[stage, 0]
        pltpu.make_async_copy(eight, eight, in_recv.at[stage, which]).wait()

    down = lax.broadcasted_iota(jnp.int32, (384, 512), 0)
    along = lax.broadcasted_iota(jnp.int32, (384, 512), 1)
    pool = jnp.where(
        down < 256,
        jnp.where(along // 2 == down, 0.5, 0.0),
        jnp.where(along // 4 == down - 256, 0.25, 0.0),
    ).astype(jnp.bfloat16)
    along = lax.broadcasted_iota(jnp.int32, (512, 384), 1)
    down = lax.broadcasted_iota(jnp.int32, (512, 384), 0)
    unpool = jnp.where(
        along < 256,
        jnp.where(down // 2 == along, 0.5, 0.0),
        jnp.where(down // 4 == along - 256, 0.25, 0.0),
    ).astype(jnp.bfloat16)

    def quad_tiles(quad):
        fine = [L0[4 * quad + i] for i in range(4)]
        return fine, [L1[2 * quad], L1[2 * quad + 1], L2[quad]]

    def halo_copy(stage, side):
        source, target, device = ((14, 0, nxt), (3, 17, prv))[side]
        return pltpu.make_async_remote_copy(
            src_ref=kv.at[stage, :, pl.ds(source * T, 3 * T)],
            dst_ref=kv.at[stage, :, pl.ds(target * T, 3 * T)],
            send_sem=halo_send.at[stage, side],
            recv_sem=halo_recv.at[stage, side],
            device_id=device,
            device_id_type=MESH,
        )

    def back_copy(stage, side, which):
        return pltpu.make_async_remote_copy(
            src_ref=grad_send.at[stage, side, which],
            dst_ref=grad_recv.at[stage, side, which],
            send_sem=back_send.at[stage, side, which],
            recv_sem=back_recv.at[stage, side, which],
            device_id=(prv, nxt)[side],
            device_id_type=MESH,
        )

    def send_out(stage, arrays, steps):
        for which in arrays:
            part = which // 2
            for step in steps:
                source = result.at[stage, which, rows_of(peers[step])]
                target = outputs[which].at[:, columns(0, stage)]
                if step == 0:
                    pltpu.make_async_copy(source, target, out_recv.at[stage, part]).start()
                    continue
                pltpu.make_async_remote_copy(
                    src_ref=source,
                    dst_ref=target,
                    send_sem=out_send.at[stage, part],
                    recv_sem=out_recv.at[stage, part],
                    device_id=(seq, peers[step]),
                    device_id_type=MESH,
                ).start()

    def prepare(stage):
        for which in range(2):
            wait_in(stage, which)
            if stage == 0:
                send_in(which, 3 if which == 0 else 0)
        for which in range(2):
            for quad in range(2):
                fine, coarse = quad_tiles(quad)
                rows = jnp.concatenate([kv[stage, which, rows_of(i)] for i in fine], axis=0)
                pooled = nn(pool, rows).astype(jnp.bfloat16)
                for at, tile in enumerate(coarse):
                    kv[stage, which, rows_of(tile)] = pooled[at * T : at * T + T]
        for side in range(2):
            halo_copy(stage, side).start()

    def compute(stage):
        for which in range(2, 4):
            wait_in(stage, which)
            if stage == 0:
                send_in(1, which - 1)
        if stage == 0:
            send_in(1, 3)
        for side in range(2):
            halo_copy(stage, side).wait()

        def one_quad(turn):
            quad = lax.rem(me // 4 + 1 + turn, 2)
            bias_prev = jnp.where((seq == 0) & (quad == 0), NEG, 0.0)
            bias_next = jnp.where((seq == groups - 1) & (quad == 1), NEG, 0.0)
            for pair in range(2):
                names = []
                for table, at0, at1 in (
                    [(L0, 2 * pair + i, 4 + 2 * pair + i) for i in (-1, 0, 1, 2)]
                    + [(L1, pair + i, 2 + pair + i) for i in (-1, 1)]
                    + [(L2, i, 1 + i) for i in (-1, 1)]
                ):
                    first, second = table[at0], table[at1]
                    names.append(first + quad * (second - first))
                keys = jnp.concatenate([kv[stage, 0, rows_of(i)] for i in names], axis=0)
                values = jnp.concatenate([kv[stage, 1, rows_of(i)] for i in names], axis=0)
                rows = pl.ds(pl.multiple_of(quad * 512 + pair * 256, 256), 256)
                attended, query_grad, key_terms, value_terms = pair_terms(
                    pair, qg[stage, 0, rows], qg[stage, 1, rows], keys, values, bias_prev, bias_next
                )
                result[stage, 0, rows] = attended
                result[stage, 1, rows] = query_grad
                for at, tile in enumerate(names):
                    acc[stage, 0, rows_of(tile)] += key_terms[at * T : at * T + T]
                    acc[stage, 1, rows_of(tile)] += value_terms[at * T : at * T + T]

            @pl.when(turn == 0)
            def _():
                send_out(stage, (0, 1), (4, 5, 6, 7))

            @pl.when(turn == 1)
            def _():
                send_out(stage, (0, 1), (1, 2, 3, 0))

        def next_turn(turn, carry):
            one_quad(turn)
            return carry

        lax.fori_loop(0, 2, next_turn, 0)
        grad_send[stage, 0] = acc[stage, :, pl.ds(0, 3 * T)].astype(jnp.bfloat16)
        grad_send[stage, 1] = acc[stage, :, pl.ds(17 * T, 3 * T)].astype(jnp.bfloat16)
        for which in range(2):
            for side in range(2):
                back_copy(stage, side, which).start()

    def finish(stage):
        for which in range(2):
            for side, tile in ((0, 14), (1, 3)):
                back_copy(stage, side, which).wait()
                received = grad_recv[stage, side, which].astype(jnp.float32)
                acc[stage, which, pl.ds(tile * T, 3 * T)] += received
            for quad in range(2):
                fine, coarse = quad_tiles(quad)
                total = jnp.concatenate([acc[stage, which, rows_of(i)] for i in fine], axis=0)
                pooled = jnp.concatenate([acc[stage, which, rows_of(i)] for i in coarse], axis=0)
                total = total + nn(unpool, pooled.astype(jnp.bfloat16))
                if which == 0:
                    total = total * SCALE
                result[stage, 2 + which, pl.ds(quad * 512, 512)] = total.astype(jnp.bfloat16)
            send_out(stage, (2 + which,), (4, 5, 6, 7, 1, 2, 3, 0))

    prepare(0)
    compute(0)
    prepare(1)
    finish(0)
    compute(1)
    finish(1)

    for stage in range(STAGES):
        for which in range(4):
            seven = qg.at[stage, 0, pl.ds(0, 7 * T)]
            pltpu.make_async_copy(seven, seven, in_send.at[stage, which]).wait()
        for part in range(2):
            seven = result.at[stage, pl.ds(0, 2), pl.ds(0, 7 * T)]
            pltpu.make_async_copy(seven, seven, out_send.at[stage, part]).wait()
            eight = result.at[stage, pl.ds(0, 2)]
            pltpu.make_async_copy(eight, eight, out_recv.at[stage, part]).wait()


def settle(*refs):
    sources, targets, sem = refs[:4], refs[4:8], refs[8]
    copies = [
        pltpu.make_async_copy(source.at[rows], target.at[rows], sem.at[at, half])
        for at, (source, target) in enumerate(zip(sources, targets))
        for half, rows in enumerate((pl.ds(0, 64), pl.ds(64, 64)))
    ]
    for copy in copies:
        copy.start()
    for copy in copies:
        copy.wait()


def on_device(query_rows, key_rows, value_rows, out_grad):
    groups = lax.axis_size("seq")
    shape = jax.ShapeDtypeStruct(query_rows.shape, jnp.bfloat16)
    anywhere = pl.BlockSpec(memory_space=pl.ANY)
    dma = pltpu.SemaphoreType.DMA
    moved = pl.pallas_call(
        functools.partial(kernel, groups),
        out_shape=(shape,) * 4,
        in_specs=[anywhere] * 4,
        out_specs=(anywhere,) * 4,
        scratch_shapes=[
            pltpu.VMEM((STAGES, 2, TILES * T, E), jnp.bfloat16),
            pltpu.VMEM((STAGES, 2, 8 * T, E), jnp.bfloat16),
            pltpu.VMEM((STAGES, 2, TILES * T, E), jnp.float32),
            pltpu.VMEM((STAGES, 2, 2, 3 * T, E), jnp.bfloat16),
            pltpu.VMEM((STAGES, 2, 2, 3 * T, E), jnp.bfloat16),
            pltpu.VMEM((STAGES, 4, 8 * T, E), jnp.bfloat16),
            dma((STAGES, 4)),
            dma((STAGES, 4)),
            dma((STAGES, 2)),
            dma((STAGES, 2)),
            dma((STAGES, 2, 2)),
            dma((STAGES, 2, 2)),
            dma((STAGES, 2)),
            dma((STAGES, 2)),
        ],
        compiler_params=pltpu.CompilerParams(
            collective_id=0, has_side_effects=True, vmem_limit_bytes=413 * 2**17
        ),
    )(query_rows, key_rows, value_rows, out_grad)
    return pl.pallas_call(
        settle,
        out_shape=(shape,) * 4,
        in_specs=[anywhere] * 4,
        out_specs=(anywhere,) * 4,
        scratch_shapes=[dma((4, 2))],
        compiler_params=pltpu.CompilerParams(vmem_limit_bytes=2**20),
    )(*moved)


def solution(mesh):
    placed = P(("seq", "grp"), None)
    return jax.shard_map(
        on_device,
        mesh=mesh,
        in_specs=(placed,) * 4,
        out_specs=(placed,) * 4,
        check_vma=False,
    )
```
